256 devices in a mesh: atoms: 64 (over x, z, core), kern: 4 (over y).
Axes of the slice: x: 4, y: 4, z: 8, core: 2. Of those that a mesh axis runs over, the one named last changes fastest.
Arguments:
- psi: bfloat16 [4096, 4, 128, 256], P('atoms', None, 'kern'), may hold values from -0.03125 to 0.03125
- potential: float32 [64, 128, 256], P('atoms', 'kern'), may hold values from -2 to 1
- kernel: float32 [64, 3, 256, 256], P('atoms', None, 'kern'), may hold values from -0.75 to 0.75
- live_count: int32 [64], replicated, may hold values from 16 to 64, as said below
- rotation: int32 [64], replicated, may hold values from 0 to 63
- bond: int32 [64], replicated, may hold values 0 or 1
Outputs:
- ham: float32 [64, 256, 256], P('atoms', 'kern')
- kernel_new: float32 [64, 3, 256, 256], P('atoms', None, 'kern')
The draws below stay inside these ranges and needn't reach their ends.
Inputs may be any that keep to these rules, and one draw needn't show every extreme that they name: Region r has live_count[r] live atom slots; some region is full in every draw.
All inputs are finite; a program needn't handle non-finite values.
Results may differ from the reference program's by a relative error of at most 0.0003.
Values may be sent and summed in bfloat16 or wider, within the bound.
No kernel may reach another device: no remote copies, remote signals or barrier semaphores. Data moves between devices by JAX's collectives and lax.ppermute only.
A program may use at most 128 MiB of HBM per device.

```python
import jax
import jax.numpy as jnp
from jax import lax

ATOMS_REG = 64
SF_ATOM = 4
PZ = 128
PX = 16
PXY = 256
SLOTS = 1
SFR = 256
TOTAL_SLOTS = 4096
N_ATOMS = 64


def draw_live_count(key, part):
    key = jax.random.fold_in(key, 11)
    count_key, full_key = jax.random.split(key)
    counts = jax.random.randint(count_key, (N_ATOMS,), ATOMS_REG // 4, ATOMS_REG + 1)
    full_region = jax.random.randint(full_key, (), 0, N_ATOMS)
    return jnp.where(jnp.arange(N_ATOMS) == full_region, ATOMS_REG, counts).astype(jnp.int32)


def plant(array, own_key, low, largest):
    longest = array.shape.index(max(array.shape))
    spots = []
    for shift in (0, 1):
        where = [jax.random.randint(jax.random.fold_in(own_key, axis), (), 0, length) for axis, length in enumerate(array.shape)]
        where[longest] = (where[longest] + shift) % array.shape[longest]
        spots.append(tuple(where))
    return array.at[spots[0]].set(low).at[spots[1]].set(largest)


def shard_levels(own_key, shape, shards, least, top_value):
    loudness, own = 1.0, jax.random.fold_in(own_key, 6)
    for position, blocks in shards:
        steps = jnp.exp(jax.random.uniform(jax.random.fold_in(own, position), (blocks,), jnp.float32, least / len(shards), top_value / len(shards)))
        loudness = loudness * jnp.repeat(steps, shape[position] // blocks).reshape([-1 if axis == position else 1 for axis in range(len(shape))])
    return loudness


def bell_draw(stream_key, extent, spread, reach, cuts=(), held_as=jnp.bfloat16):
    level = shard_levels(stream_key, extent, cuts, -0.22, 0.18) if cuts else 1.0
    entries = jax.random.normal(stream_key, extent, jnp.float32) * spread * level
    return jnp.minimum(jnp.maximum(entries, -reach), reach).astype(held_as)


def setup_inputs(seed: int = 0) -> dict:
    seeds = jax.random.split(jax.random.key(seed), 7)
    psi = bell_draw(seeds[0], (TOTAL_SLOTS, SF_ATOM, PZ, PXY), (PZ * PXY) ** -0.5, 0.03125, ((0, 64), (2, 4)))
    potential = jnp.clip(-2.0 + 3.0 * jax.random.uniform(seeds[1], (N_ATOMS, PZ, PXY), jnp.float32) ** shard_levels(seeds[1], (N_ATOMS, PZ, PXY), ((0, 64), (1, 4)), -0.2, 0.2), -2.0, 1.0)
    kernel = bell_draw(seeds[2], (N_ATOMS, 3, SFR, SFR), ATOMS_REG ** -0.5, 0.75, ((0, 64), (2, 4)), jnp.float32)
    live_count = draw_live_count(jax.random.fold_in(seeds[6], 71), 0)
    rotation = plant(jax.random.randint(seeds[4], (N_ATOMS,), 0, ATOMS_REG), jax.random.fold_in(seeds[4], 1), 0, ATOMS_REG - 1).astype(jnp.int32)
    bond = plant((jax.random.randint(seeds[5], (N_ATOMS,), 0, 2) < 1).astype(jnp.int32), jax.random.fold_in(seeds[5], 1), 0, 1)
    return {"psi": psi, "potential": potential, "kernel": kernel, "live_count": live_count, "rotation": rotation, "bond": bond}


REACHES = ((1, 4.0 / 3.0), (2, -1.0 / 12.0))
PRECISE = lax.Precision.HIGHEST


def live_table(live_count, rotation):
    member = jnp.arange(ATOMS_REG, dtype=jnp.int32)
    shifted = (member[None, :] - rotation[:, None]) % ATOMS_REG
    alive = (shifted < live_count[:, None]).astype(jnp.float32)
    return jnp.repeat(alive, SF_ATOM, axis=1)


def plane_terms(inner_field, row_cells):
    plane_cells = inner_field.shape[-1]
    last_axis = inner_field.ndim - 1
    margin = 2 * row_cells
    padded = jnp.pad(inner_field, [(0, 0)] * last_axis + [(margin, margin)])
    column = jnp.arange(plane_cells, dtype=jnp.int32) % row_cells
    running = jnp.zeros_like(inner_field)
    for reach_cells, weight in REACHES:
        for direction in (1, -1):
            offset = direction * reach_cells
            along_x = lax.slice_in_dim(padded, margin + offset, margin + offset + plane_cells, axis=last_axis)
            inside = ((column + offset >= 0) & (column + offset < row_cells)).astype(inner_field.dtype)
            along_y = lax.slice_in_dim(padded, margin + offset * row_cells, margin + offset * row_cells + plane_cells, axis=last_axis)
            running = running + weight * (along_x * inside + along_y)
    return running


def depth_terms(extended):
    depth_cells = extended.shape[1] - 4
    running = jnp.zeros_like(lax.slice_in_dim(extended, 2, 2 + depth_cells, axis=1))
    for reach_cells, weight in REACHES:
        upper = lax.slice_in_dim(extended, 2 + reach_cells, 2 + reach_cells + depth_cells, axis=1)
        lower = lax.slice_in_dim(extended, 2 - reach_cells, 2 - reach_cells + depth_cells, axis=1)
        running = running + weight * (upper + lower)
    return running


def local_ham(extended, potential):
    depth_cells = extended.shape[1] - 4
    inner_field = lax.slice_in_dim(extended, 2, 2 + depth_cells, axis=1)
    laplace = plane_terms(inner_field, PX) + depth_terms(extended) - 7.5 * inner_field
    groups = potential.shape[0]
    field_shape = inner_field.shape
    grouped = inner_field.reshape((groups, -1) + field_shape[1:])
    kinetic = (-0.5 * laplace).reshape(grouped.shape)
    applied = kinetic + potential[:, None] * grouped
    return applied.reshape(field_shape).astype(jnp.bfloat16)


def contract_cells(left, right):
    return lax.dot_general(left, right, (((1,), (1,)), ((), ())), preferred_element_type=jnp.float32)


def products(left, right):
    return jnp.einsum("rij,rjk->rik", left, right, precision=PRECISE)


def truncated(product_one, right_rows, pattern):
    result = []
    for offset in range(3):
        running = jnp.zeros_like(product_one[0])
        for inner_offset in range(3):
            target = offset - inner_offset + 1
            if 0 <= target <= 2:
                shifted = jnp.roll(right_rows[:, target], 1 - inner_offset, axis=0)
                running = running + products(product_one[inner_offset], shifted)
        result.append(running * pattern[:, offset, None, None])
    return result


def reference(psi, potential, kernel, live_count, rotation, bond):
    live_sf = live_table(live_count, rotation)
    boxes_all = psi.reshape(N_ATOMS, N_ATOMS, SLOTS, SF_ATOM, PZ, PXY)

    def one_region(region):
        chosen = lax.dynamic_index_in_dim(boxes_all, region, axis=1, keepdims=False)
        chosen = chosen.reshape(SFR, PZ, PXY)
        row_mask = lax.dynamic_index_in_dim(live_sf, region, 0, keepdims=False).astype(jnp.bfloat16)
        region_boxes = chosen * row_mask[:, None, None]
        region_pot = lax.dynamic_index_in_dim(potential, region, 0, keepdims=True)
        extended = jnp.pad(region_boxes.astype(jnp.float32), ((0, 0), (2, 2), (0, 0)))
        h_boxes = local_ham(extended, region_pot)
        flat_boxes = region_boxes.reshape(SFR, PZ * PXY)
        flat_images = h_boxes.reshape(SFR, PZ * PXY)
        return contract_cells(flat_boxes, flat_boxes), contract_cells(flat_boxes, flat_images)

    intersection, ham = lax.map(one_region, jnp.arange(N_ATOMS).astype(jnp.int32))
    pattern = jnp.stack([jnp.roll(bond, 1), jnp.ones_like(bond), bond], axis=1).astype(jnp.float32)
    columns = jnp.stack([jnp.roll(live_sf, 1 - offset, axis=0) for offset in range(3)], axis=1)
    kernel_eff = kernel * live_sf[:, None, :, None] * columns[:, :, None, :] * pattern[:, :, None, None]
    product_one = [products(kernel_eff[:, offset], jnp.roll(intersection, 1 - offset, axis=0)) for offset in range(3)]
    second = truncated(product_one, kernel_eff, pattern)
    triple = truncated(product_one, jnp.stack(second, axis=1), pattern)
    kernel_new = 3.0 * jnp.stack(second, axis=1) - 2.0 * jnp.stack(triple, axis=1)
    return ham, kernel_new
```

```python
import functools

import jax
import jax.numpy as jnp
import numpy as np
from jax import lax
from jax.experimental import pallas as pl
from jax.experimental.pallas import tpu as pltpu
from jax.sharding import PartitionSpec as P

ATOMS_REG = 64
SF_ATOM = 4
PX = 16
SFR = ATOMS_REG * SF_ATOM
GROUP = 16
EDGE = 2

REACHES_12 = ((1, 16), (2, -1))
CENTRE_12 = -90

NT = (((1,), (1,)), ((), ()))
VMEM_LIMIT = 48 * 1024 * 1024


def tile_order():
    order = np.zeros((GROUP * GROUP, GROUP * GROUP), np.float32)
    for row in range(GROUP):
        for plane in range(GROUP):
            order[plane * GROUP + row, row * GROUP + plane] = 1.0
    return order


def plane_weights(cells):
    weights = np.zeros((cells, cells), np.float32)
    for cell in range(cells):
        weights[cell, cell] = CENTRE_12
        for reach, weight in REACHES_12:
            for step in (reach, -reach):
                if 0 <= cell % PX + step < PX:
                    weights[cell + step, cell] += weight
                if 0 <= cell + step * PX < cells:
                    weights[cell + step * PX, cell] += weight
    return weights


def gram_kernel(order_ref, box_ref, planes_ref, inter_ref, low_ref, high_ref):
    rows, depth, cells = box_ref.shape
    order = order_ref[...]
    for group in range(rows // GROUP):
        own = slice(group * GROUP, (group + 1) * GROUP)
        tile = box_ref[own].reshape(GROUP * depth, cells)
        moved = jnp.dot(order, tile, preferred_element_type=jnp.float32).astype(jnp.bfloat16)
        for plane in range(depth):
            planes_ref[own, plane * cells : (plane + 1) * cells] = moved[plane * GROUP : (plane + 1) * GROUP]
    share = lax.dot_general(planes_ref[...], planes_ref[...], NT, preferred_element_type=jnp.float32)
    first = pl.program_id(0) == 0

    @pl.when(first)
    def _():
        inter_ref[...] = share
        low_ref[...] = planes_ref[:, : EDGE * cells]

    @pl.when(jnp.logical_not(first))
    def _():
        inter_ref[...] += share
        high_ref[...] = planes_ref[:, (depth - EDGE) * cells :]


def gram(boxes):
    rows, depth, cells = boxes.shape
    halves = depth // GROUP
    whole = lambda step: (0, 0)
    return pl.pallas_call(
        gram_kernel,
        grid=(halves,),
        in_specs=[
            pl.BlockSpec((GROUP * GROUP, GROUP * GROUP), whole),
            pl.BlockSpec((rows, GROUP, cells), lambda step: (0, step, 0)),
        ],
        out_specs=[
            pl.BlockSpec((rows, GROUP * cells), lambda step: (0, step)),
            pl.BlockSpec((rows, rows), whole),
            pl.BlockSpec((rows, EDGE * cells), whole),
            pl.BlockSpec((rows, EDGE * cells), whole),
        ],
        out_shape=[
            jax.ShapeDtypeStruct((rows, depth * cells), jnp.bfloat16),
            jax.ShapeDtypeStruct((rows, rows), jnp.float32),
            jax.ShapeDtypeStruct((rows, EDGE * cells), jnp.bfloat16),
            jax.ShapeDtypeStruct((rows, EDGE * cells), jnp.bfloat16),
        ],
        compiler_params=pltpu.CompilerParams(vmem_limit_bytes=VMEM_LIMIT),
        cost_estimate=pl.CostEstimate(flops=4 * rows * rows * depth * cells, bytes_accessed=4 * rows * depth * cells, transcendentals=0),
        name="gram",
    )(jnp.asarray(tile_order(), jnp.bfloat16), boxes)


def ham_kernel(weights_ref, planes_ref, below_ref, above_ref, potential_ref, ham_ref, image_ref):
    depth, cells = potential_ref.shape
    weights = weights_ref[...]

    def plane_at(plane):
        if plane < 0:
            return below_ref[:, (plane + EDGE) * cells : (plane + EDGE + 1) * cells]
        if plane >= depth:
            return above_ref[:, (plane - depth) * cells : (plane - depth + 1) * cells]
        return planes_ref[:, plane * cells : (plane + 1) * cells]

    for plane in range(depth):
        field = plane_at(plane)
        lap = jnp.dot(field, weights, preferred_element_type=jnp.float32)
        for reach, weight in REACHES_12:
            both = plane_at(plane + reach).astype(jnp.float32) + plane_at(plane - reach).astype(jnp.float32)
            lap = lap + weight * both
        image = lap * (-1.0 / 24.0) + potential_ref[plane : plane + 1, :] * field.astype(jnp.float32)
        image_ref[:, plane * cells : (plane + 1) * cells] = image.astype(jnp.bfloat16)
    ham_ref[...] = lax.dot_general(planes_ref[...], image_ref[...], NT, preferred_element_type=jnp.float32)


def hamiltonian(planes, below, above, potential):
    rows = planes.shape[0]
    depth, cells = potential.shape
    return pl.pallas_call(
        ham_kernel,
        out_shape=jax.ShapeDtypeStruct((rows, rows), jnp.float32),
        in_specs=[pl.BlockSpec(memory_space=pltpu.VMEM)] * 5,
        out_specs=pl.BlockSpec(memory_space=pltpu.VMEM),
        scratch_shapes=[pltpu.VMEM(planes.shape, jnp.bfloat16)],
        compiler_params=pltpu.CompilerParams(vmem_limit_bytes=VMEM_LIMIT),
        cost_estimate=pl.CostEstimate(flops=4 * rows * rows * depth * cells, bytes_accessed=2 * rows * depth * cells, transcendentals=0),
        name="ham",
    )(jnp.asarray(plane_weights(cells), jnp.bfloat16), planes, below, above, potential)


def halves_of(value):
    high = value.astype(jnp.bfloat16)
    return high, (value - high.astype(jnp.float32)).astype(jnp.bfloat16)


def split_kernel(value_ref, high_ref, low_ref):
    high_ref[...], low_ref[...] = halves_of(value_ref[...])


def split(blocks):
    return pl.pallas_call(
        split_kernel,
        grid=(blocks.shape[0],),
        in_specs=[pl.BlockSpec((1,) + blocks.shape[1:], lambda step: (step, 0, 0))],
        out_specs=[pl.BlockSpec((1,) + blocks.shape[1:], lambda step: (step, 0, 0))] * 2,
        out_shape=[jax.ShapeDtypeStruct(blocks.shape, jnp.bfloat16)] * 2,
        name="split",
    )(blocks)


def times(left, high, low):
    count = left.shape[0]
    left_high, left_low = halves_of(left)
    both = jnp.dot(jnp.concatenate([left_high, left_low], axis=0), high, preferred_element_type=jnp.float32)
    return both[:count] + both[count:] + jnp.dot(left_high, low, preferred_element_type=jnp.float32)


BLOCK_AT = {
    (-1, -1): 0, (-1, 0): 1, (-1, 1): 2,
    (0, -1): 3, (0, 0): 4, (0, 1): 5,
    (1, -1): 6, (1, 0): 7, (1, 1): 8,
    (-2, 1): 9, (2, -1): 10,
}
NEAR = (-1, 0, 1)


def purify_kernel(bond_ref, slab_ref, high_ref, low_ref, s_m2, s_m1, s_0, s_p1, s_p2, row_ref, column_ref, out_ref):
    bonds = {place - 2: bond_ref[place] for place in range(4)}

    def pattern(region, offset):
        return 1.0 if offset == 0 else bonds[region + min(offset, 0)]

    overlap = {place: halves_of(ref[...]) for place, ref in zip(range(-2, 3), (s_m2, s_m1, s_0, s_p1, s_p2))}

    def by_block(left, region, offset):
        place = BLOCK_AT[region, offset]
        return times(left, high_ref[place], low_ref[place])

    rows = slab_ref.shape[1]
    first = {e: times(slab_ref[e + 1] * pattern(0, e), *overlap[e]) for e in NEAR}
    chain = {(e, f): by_block(first[e], e, f) * pattern(e, f) for e in NEAR for f in NEAR}
    longer = {}
    for h in range(-2, 3):
        members = [(e, h - e) for e in NEAR if h - e in NEAR]
        product = times(jnp.concatenate([chain[m] for m in members], axis=0), *overlap[h])
        for place, member in enumerate(members):
            longer[member] = product[place * rows : (place + 1) * rows]
    for d in NEAR:
        second = sum(chain[e, d - e] for e in NEAR if d - e in NEAR)
        triple = jnp.zeros_like(second)
        for h in range(-2, 3):
            if d - h not in NEAR:
                continue
            left = sum(longer[e, h - e] * pattern(e, d - e) for e in NEAR if h - e in NEAR and d - e in NEAR)
            triple = triple + by_block(left * pattern(h, d - h), h, d - h)
        kept = row_ref[...] * column_ref[d + 1 : d + 2, :] * pattern(0, d)
        out_ref[d + 1] = (3.0 * second - 2.0 * triple) * kept


def purify(bonds, slab, high, low, overlaps, row_live, column_live):
    vmem = pl.BlockSpec(memory_space=pltpu.VMEM)
    return pl.pallas_call(
        purify_kernel,
        out_shape=jax.ShapeDtypeStruct(slab.shape, jnp.float32),
        in_specs=[pl.BlockSpec(memory_space=pltpu.SMEM)] + [vmem] * 10,
        out_specs=vmem,
        compiler_params=pltpu.CompilerParams(vmem_limit_bytes=VMEM_LIMIT),
        name="purify",
    )(bonds, slab, high, low, *overlaps, row_live, column_live)


def live_table(live_count, rotation):
    member = jnp.arange(ATOMS_REG, dtype=jnp.int32)
    shifted = (member[None, :] - rotation[:, None]) % ATOMS_REG
    alive = (shifted < live_count[:, None]).astype(jnp.float32)
    return jnp.repeat(alive, SF_ATOM, axis=1)


def moved(block, axis, by):
    count = lax.axis_size(axis)
    return lax.ppermute(block, axis, [(place, (place + by) % count) for place in range(count)])


def shards(psi, potential, kernel, live_count, rotation, bond):
    atom_count = lax.axis_size("atoms")
    kern_count = lax.axis_size("kern")
    region = lax.axis_index("atoms")
    kern_pos = lax.axis_index("kern")
    depth, cells = psi.shape[2:]
    own_rows = kernel.shape[2]

    got = lax.all_to_all(psi, "atoms", split_axis=0, concat_axis=0, tiled=True)

    slab = kernel[0]
    before = moved(slab, "atoms", 1)
    after = moved(slab, "atoms", -1)
    before_two = moved(slab[2:], "atoms", 2)
    after_two = moved(slab[:1], "atoms", -2)
    stack = jnp.concatenate([before, slab, after, before_two, after_two], axis=0)
    others = [moved(stack, "kern", by) for by in range(1, kern_count)]
    blocks = jnp.zeros((stack.shape[0], kern_count) + stack.shape[1:], stack.dtype)
    for by, part in enumerate([stack] + others):
        blocks = lax.dynamic_update_slice_in_dim(blocks, part[:, None], (kern_pos - by) % kern_count, 1)
    high, low = split(blocks.reshape(stack.shape[0], SFR, SFR))

    live_sf = live_table(live_count, rotation)
    near_live = jnp.stack([lax.dynamic_index_in_dim(live_sf, (region + e) % atom_count, 0, keepdims=False) for e in NEAR])
    my_live = near_live[1]
    row_live = lax.dynamic_slice_in_dim(my_live, kern_pos * own_rows, own_rows, 0)
    bonds = jnp.stack([lax.dynamic_index_in_dim(bond, (region + e) % atom_count, 0, keepdims=False) for e in range(-2, 2)]).astype(jnp.float32)

    planes, inter, low_edge, high_edge = gram(got.reshape(SFR, depth, cells))
    inter = inter + sum(moved(inter, "kern", by) for by in range(1, kern_count))
    inter = inter * my_live[:, None] * my_live[None, :]
    overlaps = [moved(inter, "atoms", -e) if e else inter for e in range(-2, 3)]

    up = [(place, place + 1) for place in range(kern_count - 1)]
    below = lax.ppermute(high_edge, "kern", up)
    above = lax.ppermute(low_edge, "kern", [(target, source) for source, target in up])
    ham = hamiltonian(planes, below, above, potential[0])

    def rows_of(place):
        return lax.dynamic_slice_in_dim(ham, (place % kern_count) * own_rows, own_rows, 0)

    ham_mine = rows_of(kern_pos) + sum(moved(rows_of(kern_pos + by), "kern", by) for by in range(1, kern_count))
    ham_mine = ham_mine * row_live[:, None] * my_live[None, :]

    kernel_new = purify(bonds, slab, high, low, overlaps, row_live[:, None], near_live)
    return (ham_mine[None], kernel_new[None])


def solution(mesh):
    in_specs = (
        P("atoms", None, "kern", None),
        P("atoms", "kern", None),
        P("atoms", None, "kern", None),
        P(),
        P(),
        P(),
    )
    out_specs = (P("atoms", "kern", None), P("atoms", None, "kern", None))
    return jax.shard_map(shards, mesh=mesh, in_specs=in_specs, out_specs=out_specs, check_vma=False)
```

```python
import functools

import jax
import jax.numpy as jnp
import numpy as np
from jax import lax
from jax.experimental import pallas as pl
from jax.experimental.pallas import tpu as pltpu
from jax.sharding import PartitionSpec as P

ATOMS_REG = 64
SF_ATOM = 4
PX = 16
SFR = ATOMS_REG * SF_ATOM
GROUP = 16
EDGE = 2

REACHES_12 = ((1, 16), (2, -1))
CENTRE_12 = -90

NT = (((1,), (1,)), ((), ()))
MIB = 1024 * 1024


def plane_weights(cells):
    weights = np.zeros((cells, cells), np.float32)
    for cell in range(cells):
        weights[cell, cell] = CENTRE_12
        for reach, weight in REACHES_12:
            for step in (reach, -reach):
                if 0 <= cell % PX + step < PX:
                    weights[cell + step, cell] += weight
                if 0 <= cell + step * PX < cells:
                    weights[cell + step * PX, cell] += weight
    return weights


def packed(top, corner):
    half = corner.shape[0]
    block = half // 2
    strip = corner[:block]
    return [
        top[:block],
        jnp.concatenate([corner[block:, block:], top[block:, block:]], axis=1),
        jnp.concatenate([strip[: block // 2], strip[block // 2 :]], axis=1),
    ]


def unpacked(value):
    columns = value.shape[1]
    half, block = columns // 2, columns // 4
    first, middle, last = value[:block], value[block : 2 * block], value[2 * block :]
    strip = jnp.concatenate([last[:, :half], last[:, half:]], axis=0)
    second = jnp.concatenate([first[:, block:half].T, middle[:, block:]], axis=1)
    side = jnp.concatenate([first[:, half:], second[:, half:]], axis=0).T
    corner = jnp.concatenate([strip, jnp.concatenate([strip[:, block:].T, middle[:, :block]], axis=1)], axis=0)
    return jnp.concatenate([first, second, jnp.concatenate([side, corner], axis=1)], axis=0)


def by_planes(box_ref, planes_ref, start):
    rows, depth, cells = box_ref.shape
    for group in range(rows // GROUP):
        own = slice(group * GROUP, (group + 1) * GROUP)
        tile = jnp.swapaxes(box_ref[own], 0, 1)
        for plane in range(depth):
            planes_ref[own, start + plane * cells : start + (plane + 1) * cells] = tile[plane]


def gram_kernel(box_ref, inter_ref, planes_ref):
    rows = box_ref.shape[0]
    by_planes(box_ref, planes_ref, 0)
    upper, lower = planes_ref[: rows // 2], planes_ref[rows // 2 :]
    top = lax.dot_general(upper, planes_ref[...], NT, preferred_element_type=jnp.float32)
    corner = lax.dot_general(lower, lower, NT, preferred_element_type=jnp.float32)
    share = jnp.concatenate(packed(top, corner), axis=0)
    first = pl.program_id(0) == 0

    @pl.when(first)
    def _():
        inter_ref[...] = share

    @pl.when(jnp.logical_not(first))
    def _():
        inter_ref[...] += share


def gram(boxes):
    rows, depth, cells = boxes.shape
    kept = rows * 5 // 8
    return pl.pallas_call(
        gram_kernel,
        grid=(depth // GROUP,),
        in_specs=[pl.BlockSpec((rows, GROUP, cells), lambda step: (0, step, 0))],
        out_specs=pl.BlockSpec((kept, rows), lambda step: (0, 0)),
        out_shape=jax.ShapeDtypeStruct((kept, rows), jnp.float32),
        scratch_shapes=[pltpu.VMEM((rows, GROUP * cells), jnp.bfloat16)],
        compiler_params=pltpu.CompilerParams(vmem_limit_bytes=16 * MIB),
        cost_estimate=pl.CostEstimate(flops=2 * rows * rows * depth * cells, bytes_accessed=2 * rows * depth * cells, transcendentals=0),
        name="gram",
    )(boxes)


def image_of(plane_at, plane, weights, potential):
    field = plane_at(plane)
    lap = jnp.dot(field, weights, preferred_element_type=jnp.float32)
    for reach, weight in REACHES_12:
        both = plane_at(plane + reach).astype(jnp.float32) + plane_at(plane - reach).astype(jnp.float32)
        lap = lap + weight * both
    return (lap * (-1.0 / 24.0) + potential * field.astype(jnp.float32)).astype(jnp.bfloat16)


def inner_kernel(place_ref, weights_ref, box_ref, potential_ref, ham_ref, near_ref, far_ref, rims_ref, planes_ref, image_ref):
    depth, cells = potential_ref.shape
    block = box_ref.shape[1]
    steps = depth // block
    edge = EDGE * cells

    for step in range(steps):

        @pl.when(pl.program_id(0) == step)
        def _():
            by_planes(box_ref, planes_ref, step * block * cells)

    @pl.when(pl.program_id(0) == steps - 1)
    def _():
        weights = weights_ref[...]
        plane_at = lambda plane: planes_ref[:, plane * cells : (plane + 1) * cells]
        for plane in range(EDGE, depth - EDGE):
            at = (plane - EDGE) * cells
            image_ref[:, at : at + cells] = image_of(plane_at, plane, weights, potential_ref[plane : plane + 1, :])
        inner = planes_ref[:, edge : depth * cells - edge]
        ham_ref[...] = lax.dot_general(inner, image_ref[...], NT, preferred_element_type=jnp.float32)
        low, high = planes_ref[:, :edge], planes_ref[:, depth * cells - edge :]
        rims_ref[0] = planes_ref[:, : 2 * edge]
        rims_ref[1] = planes_ref[:, depth * cells - 2 * edge :]
        odd = place_ref[1] % 2 == 1

        @pl.when(odd)
        def _():
            near_ref[...], far_ref[...] = low, high

        @pl.when(jnp.logical_not(odd))
        def _():
            near_ref[...], far_ref[...] = high, low


def ham_inner(place, boxes, potential):
    rows, depth, cells = boxes.shape
    whole = lambda step: (0, 0)
    edge = jax.ShapeDtypeStruct((rows, EDGE * cells), jnp.bfloat16)
    return pl.pallas_call(
        inner_kernel,
        grid=(depth // GROUP,),
        out_shape=[
            jax.ShapeDtypeStruct((rows, rows), jnp.float32),
            edge,
            edge,
            jax.ShapeDtypeStruct((2, rows, 2 * EDGE * cells), jnp.bfloat16),
        ],
        in_specs=[
            pl.BlockSpec(memory_space=pltpu.SMEM),
            pl.BlockSpec((cells, cells), whole),
            pl.BlockSpec((rows, GROUP, cells), lambda step: (0, step, 0)),
            pl.BlockSpec((depth, cells), whole),
        ],
        out_specs=[
            pl.BlockSpec((rows, rows), whole),
            pl.BlockSpec(edge.shape, whole),
            pl.BlockSpec(edge.shape, whole),
            pl.BlockSpec((2, rows, 2 * EDGE * cells), lambda step: (0, 0, 0)),
        ],
        scratch_shapes=[pltpu.VMEM((rows, depth * cells), jnp.bfloat16), pltpu.VMEM((rows, (depth - 2 * EDGE) * cells), jnp.bfloat16)],
        compiler_params=pltpu.CompilerParams(vmem_limit_bytes=24 * MIB),
        cost_estimate=pl.CostEstimate(flops=4 * rows * rows * depth * cells, bytes_accessed=2 * rows * depth * cells, transcendentals=0),
        name="ham_inner",
    )(place, jnp.asarray(plane_weights(cells), jnp.bfloat16), boxes, potential)


def outer_kernel(count, place_ref, weights_ref, inner_ref, near_ref, far_ref, rims_ref, potential_ref, *refs):
    slab_refs, ham_ref = refs[:-1], refs[-1]
    depth, cells = potential_ref.shape
    position = place_ref[1]
    odd = position % 2 == 1
    none = jnp.zeros_like(near_ref[...])
    below = jnp.where(position > 0, jnp.where(odd, near_ref[...], far_ref[...]), none)
    above = jnp.where(position < count - 1, jnp.where(odd, far_ref[...], near_ref[...]), none)
    weights = weights_ref[...]
    total = inner_ref[...]
    for side, (halo, start) in enumerate(((below, -EDGE), (above, depth))):
        rim_start = 0 if side == 0 else depth - 2 * EDGE

        def plane_at(plane):
            if 0 <= plane < depth:
                at = (plane - rim_start) * cells
                return rims_ref[side, :, at : at + cells]
            at = (plane - start) * cells
            return halo[:, at : at + cells]

        for plane in range(EDGE) if side == 0 else range(depth - EDGE, depth):
            image = image_of(plane_at, plane, weights, potential_ref[plane : plane + 1, :])
            total = total + lax.dot_general(plane_at(plane), image, NT, preferred_element_type=jnp.float32)
    ham_ref[...] = total
    rows = slab_refs[0].shape[0]
    for by, slab_ref in enumerate(slab_refs):
        at = pl.multiple_of(lax.bitwise_xor(position, by) * rows, rows)
        slab_ref[...] = ham_ref[pl.ds(at, rows), :]


def ham_outer(place, inner, near, far, rims, potential, count):
    rows = inner.shape[0]
    cells = potential.shape[1]
    vmem = pl.BlockSpec(memory_space=pltpu.VMEM)
    return pl.pallas_call(
        functools.partial(outer_kernel, count),
        out_shape=[jax.ShapeDtypeStruct((rows // count, rows), jnp.float32)] * count,
        in_specs=[pl.BlockSpec(memory_space=pltpu.SMEM)] + [vmem] * 6,
        out_specs=[vmem] * count,
        scratch_shapes=[pltpu.VMEM((rows, rows), jnp.float32)],
        compiler_params=pltpu.CompilerParams(vmem_limit_bytes=16 * MIB),
        name="ham_outer",
    )(place, jnp.asarray(plane_weights(cells), jnp.bfloat16), inner, near, far, rims, potential)


def halves_of(value):
    high = value.astype(jnp.bfloat16)
    return high, (value - high.astype(jnp.float32)).astype(jnp.bfloat16)


def assemble_kernel(place_ref, *refs):
    part_refs, out_ref = refs[:-1], refs[-1]
    rows = part_refs[0].shape[1]
    for by, part_ref in enumerate(part_refs):
        at = pl.multiple_of(lax.bitwise_xor(place_ref[1], by) * rows, rows)
        for block in range(part_ref.shape[0]):
            high, low = halves_of(part_ref[block])
            out_ref[2 * block, pl.ds(at, rows), :] = high
            out_ref[2 * block + 1, pl.ds(at, rows), :] = low


def assemble(place, parts):
    blocks, rows, columns = parts[0].shape
    vmem = pl.BlockSpec(memory_space=pltpu.VMEM)
    return pl.pallas_call(
        assemble_kernel,
        out_shape=jax.ShapeDtypeStruct((2 * blocks, rows * len(parts), columns), jnp.bfloat16),
        in_specs=[pl.BlockSpec(memory_space=pltpu.SMEM)] + [vmem] * len(parts),
        out_specs=vmem,
        compiler_params=pltpu.CompilerParams(vmem_limit_bytes=16 * MIB),
        name="assemble",
    )(place, *parts)


def times(left, high, low):
    count = left.shape[0]
    left_high, left_low = halves_of(left)
    both = jnp.dot(jnp.concatenate([left_high, left_low], axis=0), high, preferred_element_type=jnp.float32)
    return both[:count] + both[count:] + jnp.dot(left_high, low, preferred_element_type=jnp.float32)


NEAR = (-1, 0, 1)
REACH = range(-2, 3)


def live_atoms(position, count, rotation):
    shifted = lax.rem(position // SF_ATOM - rotation + ATOMS_REG, ATOMS_REG)
    return (shifted < count).astype(jnp.float32)


def finish_kernel(place_ref, count_ref, rotation_ref, *refs):
    part_refs, out_ref = refs[:-1], refs[-1]
    rows, columns = out_ref.shape
    count, rotation = count_ref[place_ref[0]], rotation_ref[place_ref[0]]
    own_rows = lax.broadcasted_iota(jnp.int32, (rows, 1), 0) + place_ref[1] * rows
    lanes = lax.broadcasted_iota(jnp.int32, (1, columns), 1)
    kept = live_atoms(own_rows, count, rotation) * live_atoms(lanes, count, rotation)
    out_ref[...] = sum(ref[...] for ref in part_refs) * kept


def finish(place, live_count, rotation, parts):
    smem, vmem = pl.BlockSpec(memory_space=pltpu.SMEM), pl.BlockSpec(memory_space=pltpu.VMEM)
    return pl.pallas_call(
        finish_kernel,
        out_shape=jax.ShapeDtypeStruct(parts[0].shape, jnp.float32),
        in_specs=[smem] * 3 + [vmem] * len(parts),
        out_specs=vmem,
        name="finish",
    )(place, live_count, rotation, *parts)


def purify_kernel(place_ref, count_ref, rotation_ref, bond_ref, slab_ref, *refs):
    blocks_ref, out_ref = refs[0], refs[6]
    own, core, cross, even_pair, odd_pair = (ref[...] for ref in refs[1:6])
    odd_region, odd_chip = place_ref[0] % 2 == 1, place_ref[0] // 2 % 2 == 1
    shares = {
        -2: jnp.where(odd_chip, even_pair, odd_pair),
        -1: jnp.where(odd_region, core, cross),
        0: own,
        1: jnp.where(odd_region, cross, core),
        2: jnp.where(odd_chip, odd_pair, even_pair),
    }
    regions = count_ref.shape[0]
    rows, columns = slab_ref.shape[1:]

    def at(e):
        return lax.rem(place_ref[0] + e + regions, regions)

    bonds = {e: bond_ref[at(e)].astype(jnp.float32) for e in range(-2, 2)}
    lanes = lax.broadcasted_iota(jnp.int32, (1, columns), 1)
    live = {e: live_atoms(lanes, count_ref[at(e)], rotation_ref[at(e)]) for e in REACH}
    own_rows = lax.broadcasted_iota(jnp.int32, (rows, 1), 0) + place_ref[1] * rows
    row_live = live_atoms(own_rows, count_ref[at(0)], rotation_ref[at(0)])

    def pattern(region, offset):
        return 1.0 if offset == 0 else bonds[region + min(offset, 0)]

    overlap = {e: halves_of(unpacked(shares[e])) for e in REACH}

    def by_block(left, region, offset):
        block = {-2: 0, 2: 10}.get(region, 5 + 3 * region + offset)
        return times(left, blocks_ref[2 * block], blocks_ref[2 * block + 1])

    first = {e: times(slab_ref[e + 1] * (live[e] * pattern(0, e)), *overlap[e]) * live[e] for e in NEAR}
    chain = {(e, f): by_block(first[e], e, f) * (live[e + f] * pattern(e, f)) for e in NEAR for f in NEAR}
    longer = {}
    for h in REACH:
        members = [(e, h - e) for e in NEAR if h - e in NEAR]
        product = times(jnp.concatenate([chain[m] for m in members], axis=0), *overlap[h]) * live[h]
        for place, member in enumerate(members):
            longer[member] = product[place * rows : (place + 1) * rows]
    for d in NEAR:
        second = sum(chain[e, d - e] for e in NEAR if d - e in NEAR)
        triple = jnp.zeros_like(second)
        for h in REACH:
            if d - h not in NEAR:
                continue
            left = sum(longer[e, h - e] * pattern(e, d - e) for e in NEAR if h - e in NEAR and d - e in NEAR)
            triple = triple + by_block(left * pattern(h, d - h), h, d - h)
        out_ref[d + 1] = (3.0 * second - 2.0 * triple) * (row_live * (live[d] * pattern(0, d)))


def purify(place, live_count, rotation, bond, slab, blocks, overlaps):
    smem, vmem = pl.BlockSpec(memory_space=pltpu.SMEM), pl.BlockSpec(memory_space=pltpu.VMEM)
    return pl.pallas_call(
        purify_kernel,
        out_shape=jax.ShapeDtypeStruct(slab.shape, jnp.float32),
        in_specs=[smem] * 4 + [vmem] * 7,
        out_specs=vmem,
        compiler_params=pltpu.CompilerParams(vmem_limit_bytes=24 * MIB),
        name="purify",
    )(place, live_count, rotation, bond, slab, blocks, *overlaps)


def swapped(block, axis, partner):
    count = lax.axis_size(axis)
    return lax.ppermute(block, axis, [(at, partner(at) % count) for at in range(count)])


def same_chip(at):
    return at ^ 1


def next_region_across(at):
    return at + 1 if at % 2 else at - 1


def even_chip_with_next(at):
    return at - 2 if at // 2 % 2 else at + 2


def odd_chip_with_next(at):
    return at + 2 if at // 2 % 2 else at - 2


def shards(psi, potential, kernel, live_count, rotation, bond):
    kern_count = lax.axis_size("kern")
    depth, cells = psi.shape[2:]
    place = jnp.stack([lax.axis_index("atoms"), lax.axis_index("kern")]).astype(jnp.int32)
    odd_region, odd_chip = place[0] % 2 == 1, place[0] // 2 % 2 == 1
    along_kern = [lambda at, by=by: at ^ by for by in range(kern_count)]

    slab = kernel[0]
    with_even, with_odd = swapped(slab, "atoms", even_chip_with_next), swapped(slab, "atoms", odd_chip_with_next)
    psi, with_even, with_odd = lax.optimization_barrier((psi, with_even, with_odd))

    got = lax.all_to_all(psi, "atoms", split_axis=0, concat_axis=0, tiled=True)

    before_two, after_two = jnp.where(odd_chip, with_even, with_odd), jnp.where(odd_chip, with_odd, with_even)
    other, beyond = swapped(jnp.stack([slab, jnp.where(odd_region, before_two, after_two)]), "atoms", same_chip)
    before, after = jnp.where(odd_region, other, beyond), jnp.where(odd_region, beyond, other)
    stack = jnp.concatenate([before_two[2:], before, slab, after, after_two[:1]], axis=0)
    blocks = assemble(place, [stack] + [swapped(stack, "kern", partner) for partner in along_kern[1:]])
    got, blocks = lax.optimization_barrier((got, blocks))

    boxes = got.reshape(-1, depth, cells)
    share = gram(boxes)
    half_sum = share + swapped(share, "kern", along_kern[1])
    inner, near, far, rims = ham_inner(place, boxes, potential[0])
    half_sum, near, far = lax.optimization_barrier((half_sum, near, far))
    inter = half_sum + swapped(half_sum, "kern", along_kern[3])
    near, far = swapped(near, "kern", along_kern[1]), swapped(far, "kern", along_kern[3])

    partners = (same_chip, next_region_across, even_chip_with_next, odd_chip_with_next)
    overlaps = [inter] + [swapped(inter, "atoms", partner) for partner in partners]
    slabs = ham_outer(place, inner, near, far, rims, potential[0], kern_count)
    parts = [slabs[0]] + [swapped(part, "kern", partner) for part, partner in zip(slabs[1:], along_kern[1:])]
    ham_mine = finish(place, live_count, rotation, parts)

    kernel_new = purify(place, live_count, rotation, bond, slab, blocks, overlaps)
    return (ham_mine[None], kernel_new[None])


def solution(mesh):
    in_specs = (
        P("atoms", None, "kern", None),
        P("atoms", "kern", None),
        P("atoms", None, "kern", None),
        P(),
        P(),
        P(),
    )
    out_specs = (P("atoms", "kern", None), P("atoms", None, "kern", None))
    return jax.shard_map(shards, mesh=mesh, in_specs=in_specs, out_specs=out_specs, check_vma=False)
```

```python
import functools

import jax
import jax.numpy as jnp
import numpy as np
from jax import lax
from jax.experimental import pallas as pl
from jax.experimental.pallas import tpu as pltpu
from jax.sharding import PartitionSpec as P

ATOMS_REG = 64
SF_ATOM = 4
PX = 16
SFR = ATOMS_REG * SF_ATOM
GROUP = 16
EDGE = 2

REACHES_12 = ((1, 16), (2, -1))
CENTRE_12 = -90

NT = (((1,), (1,)), ((), ()))
MIB = 1024 * 1024
ANY = pl.BlockSpec(memory_space=pl.ANY)


def plane_weights(cells):
    weights = np.zeros((cells, cells), np.float32)
    for cell in range(cells):
        weights[cell, cell] = CENTRE_12
        for reach, weight in REACHES_12:
            for step in (reach, -reach):
                if 0 <= cell % PX + step < PX:
                    weights[cell + step, cell] += weight
                if 0 <= cell + step * PX < cells:
                    weights[cell + step * PX, cell] += weight
    return weights


def packed(top, corner):
    half = corner.shape[0]
    block = half // 2
    strip = corner[:block]
    return [
        top[:block],
        jnp.concatenate([corner[block:, block:], top[block:, block:]], axis=1),
        jnp.concatenate([strip[: block // 2], strip[block // 2 :]], axis=1),
    ]


def unpacked(value):
    columns = value.shape[1]
    half, block = columns // 2, columns // 4
    first, middle, last = value[:block], value[block : 2 * block], value[2 * block :]
    strip = jnp.concatenate([last[:, :half], last[:, half:]], axis=0)
    second = jnp.concatenate([first[:, block:half].T, middle[:, block:]], axis=1)
    side = jnp.concatenate([first[:, half:], second[:, half:]], axis=0).T
    corner = jnp.concatenate([strip, jnp.concatenate([strip[:, block:].T, middle[:, :block]], axis=1)], axis=0)
    return jnp.concatenate([first, second, jnp.concatenate([side, corner], axis=1)], axis=0)


def by_planes(box_ref, planes_ref, start):
    rows, depth, cells = box_ref.shape
    for group in range(rows // GROUP):
        own = slice(group * GROUP, (group + 1) * GROUP)
        tile = jnp.swapaxes(box_ref[own], 0, 1)
        for plane in range(depth):
            planes_ref[own, start + plane * cells : start + (plane + 1) * cells] = tile[plane]


def gram_kernel(box_ref, *refs):
    inter_ref, planes_ref = refs[-2:]
    rows = box_ref.shape[0]
    by_planes(box_ref, planes_ref, 0)
    upper, lower = planes_ref[: rows // 2], planes_ref[rows // 2 :]
    top = lax.dot_general(upper, planes_ref[...], NT, preferred_element_type=jnp.float32)
    corner = lax.dot_general(lower, lower, NT, preferred_element_type=jnp.float32)
    share = jnp.concatenate(packed(top, corner), axis=0)
    first = pl.program_id(0) == 0

    @pl.when(first)
    def _():
        inter_ref[...] = share

    @pl.when(jnp.logical_not(first))
    def _():
        inter_ref[...] += share


def gram(boxes, ahead):
    rows, depth, cells = boxes.shape
    kept = rows * 5 // 8
    return pl.pallas_call(
        gram_kernel,
        grid=(depth // GROUP,),
        in_specs=[pl.BlockSpec((rows, GROUP, cells), lambda step: (0, step, 0))] + [ANY] * len(ahead),
        out_specs=pl.BlockSpec((kept, rows), lambda step: (0, 0)),
        out_shape=jax.ShapeDtypeStruct((kept, rows), jnp.float32),
        scratch_shapes=[pltpu.VMEM((rows, GROUP * cells), jnp.bfloat16)],
        compiler_params=pltpu.CompilerParams(vmem_limit_bytes=16 * MIB),
        cost_estimate=pl.CostEstimate(flops=2 * rows * rows * depth * cells, bytes_accessed=2 * rows * depth * cells, transcendentals=0),
        name="gram",
    )(boxes, *ahead)


def image_of(plane_at, plane, weights, potential):
    field = plane_at(plane)
    lap = jnp.dot(field, weights, preferred_element_type=jnp.float32)
    for reach, weight in REACHES_12:
        both = plane_at(plane + reach).astype(jnp.float32) + plane_at(plane - reach).astype(jnp.float32)
        lap = lap + weight * both
    return (lap * (-1.0 / 24.0) + potential * field.astype(jnp.float32)).astype(jnp.bfloat16)


def inner_kernel(place_ref, weights_ref, box_ref, potential_ref, ham_ref, near_ref, far_ref, rims_ref, planes_ref, image_ref):
    depth, cells = potential_ref.shape
    block = box_ref.shape[1]
    steps = depth // block
    edge = EDGE * cells

    for step in range(steps):

        @pl.when(pl.program_id(0) == step)
        def _():
            by_planes(box_ref, planes_ref, step * block * cells)

    @pl.when(pl.program_id(0) == steps - 1)
    def _():
        weights = weights_ref[...]
        plane_at = lambda plane: planes_ref[:, plane * cells : (plane + 1) * cells]
        for plane in range(EDGE, depth - EDGE):
            at = (plane - EDGE) * cells
            image_ref[:, at : at + cells] = image_of(plane_at, plane, weights, potential_ref[plane : plane + 1, :])
        inner = planes_ref[:, edge : depth * cells - edge]
        ham_ref[...] = lax.dot_general(inner, image_ref[...], NT, preferred_element_type=jnp.float32)
        low, high = planes_ref[:, :edge], planes_ref[:, depth * cells - edge :]
        rims_ref[0] = planes_ref[:, : 2 * edge]
        rims_ref[1] = planes_ref[:, depth * cells - 2 * edge :]
        odd = place_ref[1] % 2 == 1

        @pl.when(odd)
        def _():
            near_ref[...], far_ref[...] = low, high

        @pl.when(jnp.logical_not(odd))
        def _():
            near_ref[...], far_ref[...] = high, low


def ham_inner(place, boxes, potential):
    rows, depth, cells = boxes.shape
    whole = lambda step: (0, 0)
    edge = jax.ShapeDtypeStruct((rows, EDGE * cells), jnp.bfloat16)
    return pl.pallas_call(
        inner_kernel,
        grid=(depth // GROUP,),
        out_shape=[
            jax.ShapeDtypeStruct((rows, rows), jnp.float32),
            edge,
            edge,
            jax.ShapeDtypeStruct((2, rows, 2 * EDGE * cells), jnp.bfloat16),
        ],
        in_specs=[
            pl.BlockSpec(memory_space=pltpu.SMEM),
            pl.BlockSpec((cells, cells), whole),
            pl.BlockSpec((rows, GROUP, cells), lambda step: (0, step, 0)),
            pl.BlockSpec((depth, cells), whole),
        ],
        out_specs=[
            pl.BlockSpec((rows, rows), whole),
            pl.BlockSpec(edge.shape, whole),
            pl.BlockSpec(edge.shape, whole),
            pl.BlockSpec((2, rows, 2 * EDGE * cells), lambda step: (0, 0, 0)),
        ],
        scratch_shapes=[pltpu.VMEM((rows, depth * cells), jnp.bfloat16), pltpu.VMEM((rows, (depth - 2 * EDGE) * cells), jnp.bfloat16)],
        compiler_params=pltpu.CompilerParams(vmem_limit_bytes=24 * MIB),
        cost_estimate=pl.CostEstimate(flops=4 * rows * rows * depth * cells, bytes_accessed=2 * rows * depth * cells, transcendentals=0),
        name="ham_inner",
    )(place, jnp.asarray(plane_weights(cells), jnp.bfloat16), boxes, potential)


def outer_kernel(count, place_ref, weights_ref, inner_ref, near_ref, far_ref, rims_ref, potential_ref, *refs):
    slab_refs, ham_ref = refs[:-1], refs[-1]
    depth, cells = potential_ref.shape
    position = place_ref[1]
    odd = position % 2 == 1
    none = jnp.zeros_like(near_ref[...])
    below = jnp.where(position > 0, jnp.where(odd, near_ref[...], far_ref[...]), none)
    above = jnp.where(position < count - 1, jnp.where(odd, far_ref[...], near_ref[...]), none)
    weights = weights_ref[...]
    total = inner_ref[...]
    for side, (halo, start) in enumerate(((below, -EDGE), (above, depth))):
        rim_start = 0 if side == 0 else depth - 2 * EDGE

        def plane_at(plane):
            if 0 <= plane < depth:
                at = (plane - rim_start) * cells
                return rims_ref[side, :, at : at + cells]
            at = (plane - start) * cells
            return halo[:, at : at + cells]

        for plane in range(EDGE) if side == 0 else range(depth - EDGE, depth):
            image = image_of(plane_at, plane, weights, potential_ref[plane : plane + 1, :])
            total = total + lax.dot_general(plane_at(plane), image, NT, preferred_element_type=jnp.float32)
    ham_ref[...] = total
    rows = slab_refs[0].shape[0]
    for by, slab_ref in enumerate(slab_refs):
        at = pl.multiple_of(lax.bitwise_xor(position, by) * rows, rows)
        slab_ref[...] = ham_ref[pl.ds(at, rows), :]


def ham_outer(place, inner, near, far, rims, potential, count):
    rows = inner.shape[0]
    cells = potential.shape[1]
    vmem = pl.BlockSpec(memory_space=pltpu.VMEM)
    return pl.pallas_call(
        functools.partial(outer_kernel, count),
        out_shape=[jax.ShapeDtypeStruct((rows // count, rows), jnp.float32)] * count,
        in_specs=[pl.BlockSpec(memory_space=pltpu.SMEM)] + [vmem] * 6,
        out_specs=[vmem] * count,
        scratch_shapes=[pltpu.VMEM((rows, rows), jnp.float32)],
        compiler_params=pltpu.CompilerParams(vmem_limit_bytes=10 * MIB),
        name="ham_outer",
    )(place, jnp.asarray(plane_weights(cells), jnp.bfloat16), inner, near, far, rims, potential)


def outward_kernel(place_ref, blocks_ref, *refs):
    odd = place_ref[0] % 2 == 1
    count = refs[-1].shape[0]
    refs[-1][...] = jnp.where(odd, blocks_ref[:count], blocks_ref[-count:])


def outward(place, blocks, ahead):
    vmem = pl.BlockSpec(memory_space=pltpu.VMEM)
    return pl.pallas_call(
        outward_kernel,
        out_shape=jax.ShapeDtypeStruct((2,) + blocks.shape[1:], blocks.dtype),
        in_specs=[pl.BlockSpec(memory_space=pltpu.SMEM), vmem] + [ANY] * len(ahead),
        out_specs=vmem,
        compiler_params=pltpu.CompilerParams(vmem_limit_bytes=4 * MIB),
        name="outward",
    )(place, blocks, *ahead)


def pick_kernel(place_ref, even_ref, odd_ref, *refs):
    even = place_ref[0] % 2 == place_ref[0] // 2 % 2
    refs[-1][...] = jnp.where(even, even_ref[...], odd_ref[...])


def pick(place, even, odd, ahead):
    vmem = pl.BlockSpec(memory_space=pltpu.VMEM)
    return pl.pallas_call(
        pick_kernel,
        out_shape=jax.ShapeDtypeStruct(even.shape, even.dtype),
        in_specs=[pl.BlockSpec(memory_space=pltpu.SMEM), vmem, vmem] + [ANY] * len(ahead),
        out_specs=vmem,
        compiler_params=pltpu.CompilerParams(vmem_limit_bytes=4 * MIB),
        name="pick",
    )(place, even, odd, *ahead)


def total_kernel(count, *refs):
    refs[-1][...] = sum(ref[...] for ref in refs[:count])


def total(parts, ahead):
    vmem = pl.BlockSpec(memory_space=pltpu.VMEM)
    return pl.pallas_call(
        functools.partial(total_kernel, len(parts)),
        out_shape=jax.ShapeDtypeStruct(parts[0].shape, parts[0].dtype),
        in_specs=[vmem] * len(parts) + [ANY] * len(ahead),
        out_specs=vmem,
        compiler_params=pltpu.CompilerParams(vmem_limit_bytes=4 * MIB),
        name="total",
    )(*parts, *ahead)


def halves_of(value):
    high = value.astype(jnp.bfloat16)
    return high, (value - high.astype(jnp.float32)).astype(jnp.bfloat16)


def assemble_kernel(place_ref, *refs):
    part_refs, out_ref = refs[:-1], refs[-1]
    rows = part_refs[0].shape[1]
    for by, part_ref in enumerate(part_refs):
        at = pl.multiple_of(lax.bitwise_xor(place_ref[1], by) * rows, rows)
        for block in range(part_ref.shape[0]):
            high, low = halves_of(part_ref[block])
            out_ref[2 * block, pl.ds(at, rows), :] = high
            out_ref[2 * block + 1, pl.ds(at, rows), :] = low


def assemble(place, parts):
    blocks, rows, columns = parts[0].shape
    vmem = pl.BlockSpec(memory_space=pltpu.VMEM)
    return pl.pallas_call(
        assemble_kernel,
        out_shape=jax.ShapeDtypeStruct((2 * blocks, rows * len(parts), columns), jnp.bfloat16),
        in_specs=[pl.BlockSpec(memory_space=pltpu.SMEM)] + [vmem] * len(parts),
        out_specs=vmem,
        compiler_params=pltpu.CompilerParams(vmem_limit_bytes=16 * MIB),
        name="assemble",
    )(place, *parts)


def times(left, high, low):
    count = left.shape[0]
    left_high, left_low = halves_of(left)
    both = jnp.dot(jnp.concatenate([left_high, left_low], axis=0), high, preferred_element_type=jnp.float32)
    return both[:count] + both[count:] + jnp.dot(left_high, low, preferred_element_type=jnp.float32)


NEAR = (-1, 0, 1)
REACH = range(-2, 3)


def live_atoms(position, count, rotation):
    shifted = lax.rem(position // SF_ATOM - rotation + ATOMS_REG, ATOMS_REG)
    return (shifted < count).astype(jnp.float32)


def finish_kernel(place_ref, count_ref, rotation_ref, *refs):
    part_refs, out_ref = refs[:-1], refs[-1]
    rows, columns = out_ref.shape
    count, rotation = count_ref[place_ref[0]], rotation_ref[place_ref[0]]
    own_rows = lax.broadcasted_iota(jnp.int32, (rows, 1), 0) + place_ref[1] * rows
    lanes = lax.broadcasted_iota(jnp.int32, (1, columns), 1)
    kept = live_atoms(own_rows, count, rotation) * live_atoms(lanes, count, rotation)
    out_ref[...] = sum(ref[...] for ref in part_refs) * kept


def finish(place, live_count, rotation, parts):
    smem, vmem = pl.BlockSpec(memory_space=pltpu.SMEM), pl.BlockSpec(memory_space=pltpu.VMEM)
    return pl.pallas_call(
        finish_kernel,
        out_shape=jax.ShapeDtypeStruct(parts[0].shape, jnp.float32),
        in_specs=[smem] * 3 + [vmem] * len(parts),
        out_specs=vmem,
        compiler_params=pltpu.CompilerParams(vmem_limit_bytes=4 * MIB),
        name="finish",
    )(place, live_count, rotation, *parts)


def purify_kernel(place_ref, count_ref, rotation_ref, bond_ref, slab_ref, *refs):
    block_refs, out_ref = refs[5:10], refs[10]
    own, core, cross, even_pair, odd_pair = (ref[...] for ref in refs[:5])
    odd_region, odd_chip = place_ref[0] % 2 == 1, place_ref[0] // 2 % 2 == 1
    shares = {
        -2: jnp.where(odd_chip, even_pair, odd_pair),
        -1: jnp.where(odd_region, core, cross),
        0: own,
        1: jnp.where(odd_region, cross, core),
        2: jnp.where(odd_chip, odd_pair, even_pair),
    }
    regions = count_ref.shape[0]
    rows, columns = slab_ref.shape[1:]

    def at(e):
        return lax.rem(place_ref[0] + e + regions, regions)

    bonds = {e: bond_ref[at(e)].astype(jnp.float32) for e in range(-2, 2)}
    lanes = lax.broadcasted_iota(jnp.int32, (1, columns), 1)
    live = {e: live_atoms(lanes, count_ref[at(e)], rotation_ref[at(e)]) for e in REACH}
    own_rows = lax.broadcasted_iota(jnp.int32, (rows, 1), 0) + place_ref[1] * rows
    row_live = live_atoms(own_rows, count_ref[at(0)], rotation_ref[at(0)])

    def pattern(region, offset):
        return 1.0 if offset == 0 else bonds[region + min(offset, 0)]

    overlap = {e: halves_of(unpacked(shares[e])) for e in REACH}

    def by_block(left, region, offset):
        part = lambda ref, block: (ref[2 * block], ref[2 * block + 1])
        choose = lambda odd, yes, no: [jnp.where(odd, a, b) for a, b in zip(yes, no)]
        own_ref, core_ref, cross_ref, beyond_ref, behind_ref = block_refs
        if region == 0:
            return times(left, *part(own_ref, offset + 1))
        if abs(region) == 1:
            core_part, cross_part = part(core_ref, offset + 1), part(cross_ref, offset + 1)
            return times(left, *(choose(odd_region, core_part, cross_part) if region < 0 else choose(odd_region, cross_part, core_part)))
        beyond_part, behind_part = part(beyond_ref, 0), part(behind_ref, 0)
        return times(left, *(choose(odd_region, behind_part, beyond_part) if region < 0 else choose(odd_region, beyond_part, behind_part)))

    first = {e: times(slab_ref[e + 1] * (live[e] * pattern(0, e)), *overlap[e]) * live[e] for e in NEAR}
    chain = {(e, f): by_block(first[e], e, f) * (live[e + f] * pattern(e, f)) for e in NEAR for f in NEAR}
    longer = {}
    for h in REACH:
        members = [(e, h - e) for e in NEAR if h - e in NEAR]
        product = times(jnp.concatenate([chain[m] for m in members], axis=0), *overlap[h]) * live[h]
        for place, member in enumerate(members):
            longer[member] = product[place * rows : (place + 1) * rows]
    for d in NEAR:
        second = sum(chain[e, d - e] for e in NEAR if d - e in NEAR)
        triple = jnp.zeros_like(second)
        for h in REACH:
            if d - h not in NEAR:
                continue
            left = sum(longer[e, h - e] * pattern(e, d - e) for e in NEAR if h - e in NEAR and d - e in NEAR)
            triple = triple + by_block(left * pattern(h, d - h), h, d - h)
        out_ref[d + 1] = (3.0 * second - 2.0 * triple) * (row_live * (live[d] * pattern(0, d)))


def purify(place, live_count, rotation, bond, slab, overlaps, blocks):
    smem, vmem = pl.BlockSpec(memory_space=pltpu.SMEM), pl.BlockSpec(memory_space=pltpu.VMEM)
    return pl.pallas_call(
        purify_kernel,
        out_shape=jax.ShapeDtypeStruct(slab.shape, jnp.float32),
        in_specs=[smem] * 4 + [vmem] * 11,
        out_specs=vmem,
        compiler_params=pltpu.CompilerParams(vmem_limit_bytes=24 * MIB),
        name="purify",
    )(place, live_count, rotation, bond, slab, *overlaps, *blocks)


def swapped(block, axis, partner):
    count = lax.axis_size(axis)
    return lax.ppermute(block, axis, [(at, partner(at) % count) for at in range(count)])


def same_chip(at):
    return at ^ 1


def next_region_across(at):
    return at + 1 if at % 2 else at - 1


def even_chip_with_next(at):
    return at - 2 if at // 2 % 2 else at + 2


def odd_chip_with_next(at):
    return at + 2 if at // 2 % 2 else at - 2


def shards(psi, potential, kernel, live_count, rotation, bond):
    atom_count, kern_count = lax.axis_size("atoms"), lax.axis_size("kern")
    depth, cells = psi.shape[2:]
    place = jnp.stack([lax.axis_index("atoms"), lax.axis_index("kern")]).astype(jnp.int32)
    along_kern = [lambda at, by=by: at ^ by for by in range(kern_count)]

    got = lax.all_to_all(psi, "atoms", split_axis=0, concat_axis=0, tiled=True)

    slab = kernel[0]
    own = assemble(place, [slab] + [swapped(slab, "kern", partner) for partner in along_kern[1:]])
    core = swapped(own, "atoms", same_chip)
    cross = swapped(own, "atoms", next_region_across)
    away = [(at, (at - 2 if at % 2 else at + 2) % atom_count) for at in range(atom_count)]
    beyond = lax.ppermute(outward(place, own, ()), "atoms", away)
    boxes = got.reshape(-1, depth, cells)
    share = gram(boxes, (own, core))
    shares = [share] + [swapped(share, "kern", partner) for partner in along_kern[1:]]
    inner, near, far, rims = ham_inner(place, boxes, potential[0])
    near, far = swapped(near, "kern", along_kern[1]), swapped(far, "kern", along_kern[3])
    behind = swapped(outward(place, cross, (beyond, inner)), "atoms", same_chip)
    inter = total(shares, (inner,))

    near_core = swapped(inter, "atoms", same_chip)
    two_even, two_odd = swapped(inter, "atoms", even_chip_with_next), swapped(inter, "atoms", odd_chip_with_next)
    slabs = ham_outer(place, inner, near, far, rims, potential[0], kern_count)
    parts = [slabs[0]] + [swapped(part, "kern", partner) for part, partner in zip(slabs[1:], along_kern[1:])]
    ham_mine = finish(place, live_count, rotation, parts)
    across = swapped(pick(place, two_even, two_odd, (slabs[0],)), "atoms", same_chip)
    overlaps = [inter, near_core, across, two_even, two_odd]

    blocks = [own, core, cross, beyond, behind]
    kernel_new = purify(place, live_count, rotation, bond, slab, overlaps, blocks)
    return (ham_mine[None], kernel_new[None])


def solution(mesh):
    in_specs = (
        P("atoms", None, "kern", None),
        P("atoms", "kern", None),
        P("atoms", None, "kern", None),
        P(),
        P(),
        P(),
    )
    out_specs = (P("atoms", "kern", None), P("atoms", None, "kern", None))
    return jax.shard_map(shards, mesh=mesh, in_specs=in_specs, out_specs=out_specs, check_vma=False)
```

```python
import functools

import jax
import jax.numpy as jnp
import numpy as np
from jax import lax
from jax.experimental import pallas as pl
from jax.experimental.pallas import tpu as pltpu
from jax.sharding import PartitionSpec as P

ATOMS_REG = 64
SF_ATOM = 4
PX = 16
SFR = ATOMS_REG * SF_ATOM
GROUP = 16
EDGE = 2

REACHES_12 = ((1, 16), (2, -1))
CENTRE_12 = -90

NT = (((1,), (1,)), ((), ()))
MIB = 1024 * 1024
ANY = pl.BlockSpec(memory_space=pl.ANY)


def plane_weights(cells):
    weights = np.zeros((cells, cells), np.float32)
    for cell in range(cells):
        weights[cell, cell] = CENTRE_12
        for reach, weight in REACHES_12:
            for step in (reach, -reach):
                if 0 <= cell % PX + step < PX:
                    weights[cell + step, cell] += weight
                if 0 <= cell + step * PX < cells:
                    weights[cell + step * PX, cell] += weight
    return weights


def packed(top, corner):
    half = corner.shape[0]
    block = half // 2
    strip = corner[:block]
    return [
        top[:block],
        jnp.concatenate([corner[block:, block:], top[block:, block:]], axis=1),
        jnp.concatenate([strip[: block // 2], strip[block // 2 :]], axis=1),
    ]


def unpacked(value):
    columns = value.shape[1]
    half, block = columns // 2, columns // 4
    first, middle, last = value[:block], value[block : 2 * block], value[2 * block :]
    strip = jnp.concatenate([last[:, :half], last[:, half:]], axis=0)
    second = jnp.concatenate([first[:, block:half].T, middle[:, block:]], axis=1)
    side = jnp.concatenate([first[:, half:], second[:, half:]], axis=0).T
    corner = jnp.concatenate([strip, jnp.concatenate([strip[:, block:].T, middle[:, :block]], axis=1)], axis=0)
    return jnp.concatenate([first, second, jnp.concatenate([side, corner], axis=1)], axis=0)


def by_planes(box_ref, planes_ref, start):
    rows, depth, cells = box_ref.shape
    for group in range(rows // GROUP):
        own = slice(group * GROUP, (group + 1) * GROUP)
        tile = jnp.swapaxes(box_ref[own], 0, 1)
        for plane in range(depth):
            planes_ref[own, start + plane * cells : start + (plane + 1) * cells] = tile[plane]


def gram_kernel(place_ref, box_ref, *refs):
    inter_ref, near_ref, far_ref, planes_ref = refs[-4:]
    rows, depth, cells = box_ref.shape
    by_planes(box_ref, planes_ref, 0)
    upper, lower = planes_ref[: rows // 2], planes_ref[rows // 2 :]
    top = lax.dot_general(upper, planes_ref[...], NT, preferred_element_type=jnp.float32)
    corner = lax.dot_general(lower, lower, NT, preferred_element_type=jnp.float32)
    share = jnp.concatenate(packed(top, corner), axis=0)
    kept = share.shape[0]
    first = pl.program_id(0) == 0
    odd = place_ref[1] % 2 == 1

    def put(edge_ref, start):
        for edge in range(EDGE):
            at = 2 * kept + edge * rows
            edge_ref[at : at + rows] = planes_ref[:, (start + edge) * cells : (start + edge + 1) * cells]

    @pl.when(first)
    def _():
        inter_ref[...] = share

    @pl.when(jnp.logical_not(first))
    def _():
        whole = inter_ref[...] + share
        inter_ref[...] = whole
        high, low = halves_of(whole)
        for message_ref in (near_ref, far_ref):
            message_ref[:kept] = high
            message_ref[kept : 2 * kept] = low

    @pl.when(jnp.logical_and(first, odd))
    def _():
        put(near_ref, 0)

    @pl.when(jnp.logical_and(first, jnp.logical_not(odd)))
    def _():
        put(far_ref, 0)

    @pl.when(jnp.logical_and(jnp.logical_not(first), odd))
    def _():
        put(far_ref, depth - EDGE)

    @pl.when(jnp.logical_and(jnp.logical_not(first), jnp.logical_not(odd)))
    def _():
        put(near_ref, depth - EDGE)


def gram(place, boxes, ahead):
    rows, depth, cells = boxes.shape
    kept = rows * 5 // 8
    whole = lambda step: (0, 0)
    message = jax.ShapeDtypeStruct((2 * kept + EDGE * rows, cells), jnp.bfloat16)
    return pl.pallas_call(
        gram_kernel,
        grid=(depth // GROUP,),
        in_specs=[pl.BlockSpec(memory_space=pltpu.SMEM), pl.BlockSpec((rows, GROUP, cells), lambda step: (0, step, 0))] + [ANY] * len(ahead),
        out_specs=[pl.BlockSpec((kept, rows), whole), pl.BlockSpec(message.shape, whole), pl.BlockSpec(message.shape, whole)],
        out_shape=[jax.ShapeDtypeStruct((kept, rows), jnp.float32), message, message],
        scratch_shapes=[pltpu.VMEM((rows, GROUP * cells), jnp.bfloat16)],
        compiler_params=pltpu.CompilerParams(vmem_limit_bytes=16 * MIB),
        cost_estimate=pl.CostEstimate(flops=2 * rows * rows * depth * cells, bytes_accessed=2 * rows * depth * cells, transcendentals=0),
        name="gram",
    )(place, boxes, *ahead)


def image_of(plane_at, plane, weights, potential):
    field = plane_at(plane)
    lap = jnp.dot(field, weights, preferred_element_type=jnp.float32)
    for reach, weight in REACHES_12:
        both = plane_at(plane + reach).astype(jnp.float32) + plane_at(plane - reach).astype(jnp.float32)
        lap = lap + weight * both
    return (lap * (-1.0 / 24.0) + potential * field.astype(jnp.float32)).astype(jnp.bfloat16)


def inner_kernel(weights_ref, box_ref, potential_ref, ham_ref, rims_ref, planes_ref, image_ref):
    depth, cells = potential_ref.shape
    block = box_ref.shape[1]
    steps = depth // block
    edge = EDGE * cells

    for step in range(steps):

        @pl.when(pl.program_id(0) == step)
        def _():
            by_planes(box_ref, planes_ref, step * block * cells)

    @pl.when(pl.program_id(0) == steps - 1)
    def _():
        weights = weights_ref[...]
        plane_at = lambda plane: planes_ref[:, plane * cells : (plane + 1) * cells]
        for plane in range(EDGE, depth - EDGE):
            at = (plane - EDGE) * cells
            image_ref[:, at : at + cells] = image_of(plane_at, plane, weights, potential_ref[plane : plane + 1, :])
        inner = planes_ref[:, edge : depth * cells - edge]
        ham_ref[...] = lax.dot_general(inner, image_ref[...], NT, preferred_element_type=jnp.float32)
        rims_ref[0] = planes_ref[:, : 2 * edge]
        rims_ref[1] = planes_ref[:, depth * cells - 2 * edge :]


def ham_inner(boxes, potential):
    rows, depth, cells = boxes.shape
    whole = lambda step: (0, 0)
    return pl.pallas_call(
        inner_kernel,
        grid=(depth // GROUP,),
        out_shape=[
            jax.ShapeDtypeStruct((rows, rows), jnp.float32),
            jax.ShapeDtypeStruct((2, rows, 2 * EDGE * cells), jnp.bfloat16),
        ],
        in_specs=[
            pl.BlockSpec((cells, cells), whole),
            pl.BlockSpec((rows, GROUP, cells), lambda step: (0, step, 0)),
            pl.BlockSpec((depth, cells), whole),
        ],
        out_specs=[
            pl.BlockSpec((rows, rows), whole),
            pl.BlockSpec((2, rows, 2 * EDGE * cells), lambda step: (0, 0, 0)),
        ],
        scratch_shapes=[pltpu.VMEM((rows, depth * cells), jnp.bfloat16), pltpu.VMEM((rows, (depth - 2 * EDGE) * cells), jnp.bfloat16)],
        compiler_params=pltpu.CompilerParams(vmem_limit_bytes=24 * MIB),
        cost_estimate=pl.CostEstimate(flops=4 * rows * rows * depth * cells, bytes_accessed=2 * rows * depth * cells, transcendentals=0),
        name="ham_inner",
    )(jnp.asarray(plane_weights(cells), jnp.bfloat16), boxes, potential)


def outer_kernel(count, place_ref, weights_ref, inner_ref, near_ref, far_ref, rims_ref, potential_ref, *refs):
    slab_refs, ham_ref = refs[:-1], refs[-1]
    depth, cells = potential_ref.shape
    position = place_ref[1]
    odd = position % 2 == 1
    edges = near_ref.shape[0] - EDGE * inner_ref.shape[0]
    near, far = near_ref[edges:], far_ref[edges:]
    none = jnp.zeros_like(near)
    below = jnp.where(position > 0, jnp.where(odd, near, far), none)
    above = jnp.where(position < count - 1, jnp.where(odd, far, near), none)
    weights = weights_ref[...]
    total = inner_ref[...]
    for side, (halo, start) in enumerate(((below, -EDGE), (above, depth))):
        rim_start = 0 if side == 0 else depth - 2 * EDGE

        def plane_at(plane):
            if 0 <= plane < depth:
                at = (plane - rim_start) * cells
                return rims_ref[side, :, at : at + cells]
            at = (plane - start) * halo.shape[0] // EDGE
            return halo[at : at + halo.shape[0] // EDGE]

        for plane in range(EDGE) if side == 0 else range(depth - EDGE, depth):
            image = image_of(plane_at, plane, weights, potential_ref[plane : plane + 1, :])
            total = total + lax.dot_general(plane_at(plane), image, NT, preferred_element_type=jnp.float32)
    ham_ref[...] = total
    rows = slab_refs[0].shape[0]
    for by, slab_ref in enumerate(slab_refs):
        at = pl.multiple_of(lax.bitwise_xor(position, by) * rows, rows)
        slab_ref[...] = ham_ref[pl.ds(at, rows), :]


def ham_outer(place, inner, near, far, rims, potential, count):
    rows = inner.shape[0]
    cells = potential.shape[1]
    vmem = pl.BlockSpec(memory_space=pltpu.VMEM)
    return pl.pallas_call(
        functools.partial(outer_kernel, count),
        out_shape=[jax.ShapeDtypeStruct((rows // count, rows), jnp.float32)] * count,
        in_specs=[pl.BlockSpec(memory_space=pltpu.SMEM)] + [vmem] * 6,
        out_specs=[vmem] * count,
        scratch_shapes=[pltpu.VMEM((rows, rows), jnp.float32)],
        compiler_params=pltpu.CompilerParams(vmem_limit_bytes=10 * MIB),
        name="ham_outer",
    )(place, jnp.asarray(plane_weights(cells), jnp.bfloat16), inner, near, far, rims, potential)


def outward_kernel(place_ref, blocks_ref, *refs):
    odd = place_ref[0] % 2 == 1
    count = refs[-1].shape[0]
    refs[-1][...] = jnp.where(odd, blocks_ref[:count], blocks_ref[-count:])


def outward(place, blocks, ahead):
    vmem = pl.BlockSpec(memory_space=pltpu.VMEM)
    return pl.pallas_call(
        outward_kernel,
        out_shape=jax.ShapeDtypeStruct((2,) + blocks.shape[1:], blocks.dtype),
        in_specs=[pl.BlockSpec(memory_space=pltpu.SMEM), vmem] + [ANY] * len(ahead),
        out_specs=vmem,
        compiler_params=pltpu.CompilerParams(vmem_limit_bytes=4 * MIB),
        name="outward",
    )(place, blocks, *ahead)


def pick_kernel(place_ref, own_ref, even_ref, odd_ref, *refs):
    even = place_ref[0] % 2 == place_ref[0] // 2 % 2
    refs[-1][0] = own_ref[...]
    refs[-1][1] = jnp.where(even, even_ref[...], odd_ref[...])


def pick(place, own, even, odd, ahead):
    vmem = pl.BlockSpec(memory_space=pltpu.VMEM)
    return pl.pallas_call(
        pick_kernel,
        out_shape=jax.ShapeDtypeStruct((2,) + own.shape, own.dtype),
        in_specs=[pl.BlockSpec(memory_space=pltpu.SMEM), vmem, vmem, vmem] + [ANY] * len(ahead),
        out_specs=vmem,
        compiler_params=pltpu.CompilerParams(vmem_limit_bytes=4 * MIB),
        name="pick",
    )(place, own, even, odd, *ahead)


def total_kernel(own_ref, across_ref, near_ref, far_ref, *refs):
    kept = own_ref.shape[0]
    whole = own_ref[...] + across_ref[...]
    for message_ref in (near_ref, far_ref):
        whole = whole + (message_ref[:kept].astype(jnp.float32) + message_ref[kept : 2 * kept].astype(jnp.float32))
    refs[-1][...] = whole


def total(own, across, near, far, ahead):
    vmem = pl.BlockSpec(memory_space=pltpu.VMEM)
    return pl.pallas_call(
        total_kernel,
        out_shape=jax.ShapeDtypeStruct(own.shape, own.dtype),
        in_specs=[vmem] * 4 + [ANY] * len(ahead),
        out_specs=vmem,
        compiler_params=pltpu.CompilerParams(vmem_limit_bytes=4 * MIB),
        name="total",
    )(own, across, near, far, *ahead)


def halves_of(value):
    high = value.astype(jnp.bfloat16)
    return high, (value - high.astype(jnp.float32)).astype(jnp.bfloat16)


def assemble_kernel(place_ref, *refs):
    part_refs, out_ref = refs[:-1], refs[-1]
    rows = part_refs[0].shape[1]
    for by, part_ref in enumerate(part_refs):
        at = pl.multiple_of(lax.bitwise_xor(place_ref[1], by) * rows, rows)
        for block in range(part_ref.shape[0]):
            high, low = halves_of(part_ref[block])
            out_ref[2 * block, pl.ds(at, rows), :] = high
            out_ref[2 * block + 1, pl.ds(at, rows), :] = low


def assemble(place, parts):
    blocks, rows, columns = parts[0].shape
    vmem = pl.BlockSpec(memory_space=pltpu.VMEM)
    return pl.pallas_call(
        assemble_kernel,
        out_shape=jax.ShapeDtypeStruct((2 * blocks, rows * len(parts), columns), jnp.bfloat16),
        in_specs=[pl.BlockSpec(memory_space=pltpu.SMEM)] + [vmem] * len(parts),
        out_specs=vmem,
        compiler_params=pltpu.CompilerParams(vmem_limit_bytes=16 * MIB),
        name="assemble",
    )(place, *parts)


def times(left, high, low):
    count = left.shape[0]
    left_high, left_low = halves_of(left)
    both = jnp.dot(jnp.concatenate([left_high, left_low], axis=0), high, preferred_element_type=jnp.float32)
    return both[:count] + both[count:] + jnp.dot(left_high, low, preferred_element_type=jnp.float32)


NEAR = (-1, 0, 1)
REACH = range(-2, 3)


def live_atoms(position, count, rotation):
    shifted = lax.rem(position // SF_ATOM - rotation + ATOMS_REG, ATOMS_REG)
    return (shifted < count).astype(jnp.float32)


def finish_kernel(parts, place_ref, count_ref, rotation_ref, *refs):
    part_refs, out_ref = refs[:parts], refs[-1]
    rows, columns = out_ref.shape
    count, rotation = count_ref[place_ref[0]], rotation_ref[place_ref[0]]
    own_rows = lax.broadcasted_iota(jnp.int32, (rows, 1), 0) + place_ref[1] * rows
    lanes = lax.broadcasted_iota(jnp.int32, (1, columns), 1)
    kept = live_atoms(own_rows, count, rotation) * live_atoms(lanes, count, rotation)
    out_ref[...] = sum(ref[...] for ref in part_refs) * kept


def finish(place, live_count, rotation, parts, ahead):
    smem, vmem = pl.BlockSpec(memory_space=pltpu.SMEM), pl.BlockSpec(memory_space=pltpu.VMEM)
    return pl.pallas_call(
        functools.partial(finish_kernel, len(parts)),
        out_shape=jax.ShapeDtypeStruct(parts[0].shape, jnp.float32),
        in_specs=[smem] * 3 + [vmem] * len(parts) + [ANY] * len(ahead),
        out_specs=vmem,
        compiler_params=pltpu.CompilerParams(vmem_limit_bytes=4 * MIB),
        name="finish",
    )(place, live_count, rotation, *parts, *ahead)


def purify_kernel(place_ref, count_ref, rotation_ref, bond_ref, slab_ref, *refs):
    block_refs, out_ref = refs[4:9], refs[9]
    own, (core, cross), even_pair, odd_pair = (ref[...] for ref in refs[:4])
    odd_region, odd_chip = place_ref[0] % 2 == 1, place_ref[0] // 2 % 2 == 1
    shares = {
        -2: jnp.where(odd_chip, even_pair, odd_pair),
        -1: jnp.where(odd_region, core, cross),
        0: own,
        1: jnp.where(odd_region, cross, core),
        2: jnp.where(odd_chip, odd_pair, even_pair),
    }
    regions = count_ref.shape[0]
    rows, columns = slab_ref.shape[1:]

    def at(e):
        return lax.rem(place_ref[0] + e + regions, regions)

    bonds = {e: bond_ref[at(e)].astype(jnp.float32) for e in range(-2, 2)}
    lanes = lax.broadcasted_iota(jnp.int32, (1, columns), 1)
    live = {e: live_atoms(lanes, count_ref[at(e)], rotation_ref[at(e)]) for e in REACH}
    own_rows = lax.broadcasted_iota(jnp.int32, (rows, 1), 0) + place_ref[1] * rows
    row_live = live_atoms(own_rows, count_ref[at(0)], rotation_ref[at(0)])

    def pattern(region, offset):
        return 1.0 if offset == 0 else bonds[region + min(offset, 0)]

    overlap = {e: halves_of(unpacked(shares[e])) for e in REACH}

    def by_block(left, region, offset):
        part = lambda ref, block: (ref[2 * block], ref[2 * block + 1])
        choose = lambda odd, yes, no: [jnp.where(odd, a, b) for a, b in zip(yes, no)]
        own_ref, core_ref, cross_ref, beyond_ref, behind_ref = block_refs
        if region == 0:
            return times(left, *part(own_ref, offset + 1))
        if abs(region) == 1:
            core_part, cross_part = part(core_ref, offset + 1), part(cross_ref, offset + 1)
            return times(left, *(choose(odd_region, core_part, cross_part) if region < 0 else choose(odd_region, cross_part, core_part)))
        beyond_part, behind_part = part(beyond_ref, 0), part(behind_ref, 0)
        return times(left, *(choose(odd_region, behind_part, beyond_part) if region < 0 else choose(odd_region, beyond_part, behind_part)))

    first = {e: times(slab_ref[e + 1] * (live[e] * pattern(0, e)), *overlap[e]) * live[e] for e in NEAR}
    chain = {(e, f): by_block(first[e], e, f) * (live[e + f] * pattern(e, f)) for e in NEAR for f in NEAR}
    longer = {}
    for h in REACH:
        members = [(e, h - e) for e in NEAR if h - e in NEAR]
        product = times(jnp.concatenate([chain[m] for m in members], axis=0), *overlap[h]) * live[h]
        for place, member in enumerate(members):
            longer[member] = product[place * rows : (place + 1) * rows]
    for d in NEAR:
        second = sum(chain[e, d - e] for e in NEAR if d - e in NEAR)
        triple = jnp.zeros_like(second)
        for h in REACH:
            if d - h not in NEAR:
                continue
            left = sum(longer[e, h - e] * pattern(e, d - e) for e in NEAR if h - e in NEAR and d - e in NEAR)
            triple = triple + by_block(left * pattern(h, d - h), h, d - h)
        out_ref[d + 1] = (3.0 * second - 2.0 * triple) * (row_live * (live[d] * pattern(0, d)))


def purify(place, live_count, rotation, bond, slab, overlaps, blocks):
    smem, vmem = pl.BlockSpec(memory_space=pltpu.SMEM), pl.BlockSpec(memory_space=pltpu.VMEM)
    return pl.pallas_call(
        purify_kernel,
        out_shape=jax.ShapeDtypeStruct(slab.shape, jnp.float32),
        in_specs=[smem] * 4 + [vmem] * 10,
        out_specs=vmem,
        compiler_params=pltpu.CompilerParams(vmem_limit_bytes=24 * MIB),
        name="purify",
    )(place, live_count, rotation, bond, slab, *overlaps, *blocks)


def swapped(block, axis, partner):
    count = lax.axis_size(axis)
    return lax.ppermute(block, axis, [(at, partner(at) % count) for at in range(count)])


def same_chip(at):
    return at ^ 1


def next_region_across(at):
    return at + 1 if at % 2 else at - 1


def even_chip_with_next(at):
    return at - 2 if at // 2 % 2 else at + 2


def odd_chip_with_next(at):
    return at + 2 if at // 2 % 2 else at - 2


def shards(psi, potential, kernel, live_count, rotation, bond):
    atom_count, kern_count = lax.axis_size("atoms"), lax.axis_size("kern")
    depth, cells = psi.shape[2:]
    place = jnp.stack([lax.axis_index("atoms"), lax.axis_index("kern")]).astype(jnp.int32)
    along_kern = [lambda at, by=by: at ^ by for by in range(kern_count)]

    got = lax.all_to_all(psi, "atoms", split_axis=0, concat_axis=0, tiled=True)

    slab = kernel[0]
    own = assemble(place, [slab] + [swapped(slab, "kern", partner) for partner in along_kern[1:]])
    core = swapped(own, "atoms", same_chip)
    cross = swapped(own, "atoms", next_region_across)
    away = [(at, (at - 2 if at % 2 else at + 2) % atom_count) for at in range(atom_count)]
    beyond = lax.ppermute(outward(place, own, ()), "atoms", away)
    boxes = got.reshape(-1, depth, cells)
    share, near, far = gram(place, boxes, (own, core))
    opposite = swapped(share, "kern", along_kern[2])
    near, far = swapped(near, "kern", along_kern[1]), swapped(far, "kern", along_kern[3])
    inner, rims = ham_inner(boxes, potential[0])
    inter = total(share, opposite, near, far, (inner, cross, beyond))
    behind = swapped(outward(place, cross, (inter,)), "atoms", same_chip)

    two_even, two_odd = swapped(inter, "atoms", even_chip_with_next), swapped(inter, "atoms", odd_chip_with_next)
    slabs = ham_outer(place, inner, near, far, rims, potential[0], kern_count)
    parts = [slabs[0]] + [swapped(part, "kern", partner) for part, partner in zip(slabs[1:], along_kern[1:])]
    picked = pick(place, inter, two_even, two_odd, parts)
    from_core = swapped(picked, "atoms", same_chip)
    ham_mine = finish(place, live_count, rotation, parts, (picked,))
    overlaps = [inter, from_core, two_even, two_odd]

    blocks = [own, core, cross, beyond, behind]
    kernel_new = purify(place, live_count, rotation, bond, slab, overlaps, blocks)
    return (ham_mine[None], kernel_new[None])


def solution(mesh):
    in_specs = (
        P("atoms", None, "kern", None),
        P("atoms", "kern", None),
        P("atoms", None, "kern", None),
        P(),
        P(),
        P(),
    )
    out_specs = (P("atoms", "kern", None), P("atoms", None, "kern", None))
    return jax.shard_map(shards, mesh=mesh, in_specs=in_specs, out_specs=out_specs, check_vma=False)
```

```python
import functools

import jax
import jax.numpy as jnp
import numpy as np
from jax import lax
from jax.experimental import pallas as pl
from jax.experimental.pallas import tpu as pltpu
from jax.sharding import PartitionSpec as P

ATOMS_REG = 64
SF_ATOM = 4
PX = 16
SFR = ATOMS_REG * SF_ATOM
GROUP = 16
EDGE = 2

REACHES_12 = ((1, 16), (2, -1))
CENTRE_12 = -90

NT = (((1,), (1,)), ((), ()))
MIB = 1024 * 1024
ANY = pl.BlockSpec(memory_space=pl.ANY)


def plane_weights(cells):
    weights = np.zeros((cells, cells), np.float32)
    for cell in range(cells):
        weights[cell, cell] = CENTRE_12
        for reach, weight in REACHES_12:
            for step in (reach, -reach):
                if 0 <= cell % PX + step < PX:
                    weights[cell + step, cell] += weight
                if 0 <= cell + step * PX < cells:
                    weights[cell + step * PX, cell] += weight
    return weights


def packed(top, corner):
    half = corner.shape[0]
    block = half // 2
    strip = corner[:block]
    return [
        top[:block],
        jnp.concatenate([corner[block:, block:], top[block:, block:]], axis=1),
        jnp.concatenate([strip[: block // 2], strip[block // 2 :]], axis=1),
    ]


def unpacked(value):
    columns = value.shape[1]
    half, block = columns // 2, columns // 4
    first, middle, last = value[:block], value[block : 2 * block], value[2 * block :]
    strip = jnp.concatenate([last[:, :half], last[:, half:]], axis=0)
    second = jnp.concatenate([first[:, block:half].T, middle[:, block:]], axis=1)
    side = jnp.concatenate([first[:, half:], second[:, half:]], axis=0).T
    corner = jnp.concatenate([strip, jnp.concatenate([strip[:, block:].T, middle[:, :block]], axis=1)], axis=0)
    return jnp.concatenate([first, second, jnp.concatenate([side, corner], axis=1)], axis=0)


def by_planes(box_ref, planes_ref, start):
    rows, depth, cells = box_ref.shape
    for group in range(rows // GROUP):
        own = slice(group * GROUP, (group + 1) * GROUP)
        tile = jnp.swapaxes(box_ref[own], 0, 1)
        for plane in range(depth):
            planes_ref[own, start + plane * cells : start + (plane + 1) * cells] = tile[plane]


def gram_kernel(place_ref, box_ref, *refs):
    inter_ref, near_ref, far_ref, planes_ref = refs[-4:]
    rows, depth, cells = box_ref.shape
    by_planes(box_ref, planes_ref, 0)
    upper, lower = planes_ref[: rows // 2], planes_ref[rows // 2 :]
    top = lax.dot_general(upper, planes_ref[...], NT, preferred_element_type=jnp.float32)
    corner = lax.dot_general(lower, lower, NT, preferred_element_type=jnp.float32)
    share = jnp.concatenate(packed(top, corner), axis=0)
    kept = share.shape[0]
    first = pl.program_id(0) == 0
    odd = place_ref[1] % 2 == 1

    def put(edge_ref, start):
        for edge in range(EDGE):
            at = 2 * kept + edge * rows
            edge_ref[at : at + rows] = planes_ref[:, (start + edge) * cells : (start + edge + 1) * cells]

    @pl.when(first)
    def _():
        inter_ref[...] = share

    @pl.when(jnp.logical_not(first))
    def _():
        whole = inter_ref[...] + share
        inter_ref[...] = whole
        high, low = halves_of(whole)
        for message_ref in (near_ref, far_ref):
            message_ref[:kept] = high
            message_ref[kept : 2 * kept] = low

    @pl.when(jnp.logical_and(first, odd))
    def _():
        put(near_ref, 0)

    @pl.when(jnp.logical_and(first, jnp.logical_not(odd)))
    def _():
        put(far_ref, 0)

    @pl.when(jnp.logical_and(jnp.logical_not(first), odd))
    def _():
        put(far_ref, depth - EDGE)

    @pl.when(jnp.logical_and(jnp.logical_not(first), jnp.logical_not(odd)))
    def _():
        put(near_ref, depth - EDGE)


def gram(place, boxes, ahead):
    rows, depth, cells = boxes.shape
    kept = rows * 5 // 8
    whole = lambda step: (0, 0)
    message = jax.ShapeDtypeStruct((2 * kept + EDGE * rows, cells), jnp.bfloat16)
    return pl.pallas_call(
        gram_kernel,
        grid=(depth // GROUP,),
        in_specs=[pl.BlockSpec(memory_space=pltpu.SMEM), pl.BlockSpec((rows, GROUP, cells), lambda step: (0, step, 0))] + [ANY] * len(ahead),
        out_specs=[pl.BlockSpec((kept, rows), whole), pl.BlockSpec(message.shape, whole), pl.BlockSpec(message.shape, whole)],
        out_shape=[jax.ShapeDtypeStruct((kept, rows), jnp.float32), message, message],
        scratch_shapes=[pltpu.VMEM((rows, GROUP * cells), jnp.bfloat16)],
        compiler_params=pltpu.CompilerParams(vmem_limit_bytes=16 * MIB),
        cost_estimate=pl.CostEstimate(flops=2 * rows * rows * depth * cells, bytes_accessed=2 * rows * depth * cells, transcendentals=0),
        name="gram",
    )(place, boxes, *ahead)


def image_of(plane_at, plane, weights, potential):
    field = plane_at(plane)
    lap = jnp.dot(field, weights, preferred_element_type=jnp.float32)
    for reach, weight in REACHES_12:
        both = plane_at(plane + reach).astype(jnp.float32) + plane_at(plane - reach).astype(jnp.float32)
        lap = lap + weight * both
    return (lap * (-1.0 / 24.0) + potential * field.astype(jnp.float32)).astype(jnp.bfloat16)


def inner_kernel(weights_ref, box_ref, potential_ref, ham_ref, rims_ref, planes_ref, image_ref):
    depth, cells = potential_ref.shape
    block = box_ref.shape[1]
    steps = depth // block
    edge = EDGE * cells

    for step in range(steps):

        @pl.when(pl.program_id(0) == step)
        def _():
            by_planes(box_ref, planes_ref, step * block * cells)

    @pl.when(pl.program_id(0) == steps - 1)
    def _():
        weights = weights_ref[...]
        plane_at = lambda plane: planes_ref[:, plane * cells : (plane + 1) * cells]
        for plane in range(EDGE, depth - EDGE):
            at = (plane - EDGE) * cells
            image_ref[:, at : at + cells] = image_of(plane_at, plane, weights, potential_ref[plane : plane + 1, :])
        inner = planes_ref[:, edge : depth * cells - edge]
        ham_ref[...] = lax.dot_general(inner, image_ref[...], NT, preferred_element_type=jnp.float32)
        rims_ref[0] = planes_ref[:, : 2 * edge]
        rims_ref[1] = planes_ref[:, depth * cells - 2 * edge :]


def ham_inner(boxes, potential):
    rows, depth, cells = boxes.shape
    whole = lambda step: (0, 0)
    return pl.pallas_call(
        inner_kernel,
        grid=(depth // GROUP,),
        out_shape=[
            jax.ShapeDtypeStruct((rows, rows), jnp.float32),
            jax.ShapeDtypeStruct((2, rows, 2 * EDGE * cells), jnp.bfloat16),
        ],
        in_specs=[
            pl.BlockSpec((cells, cells), whole),
            pl.BlockSpec((rows, GROUP, cells), lambda step: (0, step, 0)),
            pl.BlockSpec((depth, cells), whole),
        ],
        out_specs=[
            pl.BlockSpec((rows, rows), whole),
            pl.BlockSpec((2, rows, 2 * EDGE * cells), lambda step: (0, 0, 0)),
        ],
        scratch_shapes=[pltpu.VMEM((rows, depth * cells), jnp.bfloat16), pltpu.VMEM((rows, (depth - 2 * EDGE) * cells), jnp.bfloat16)],
        compiler_params=pltpu.CompilerParams(vmem_limit_bytes=24 * MIB),
        cost_estimate=pl.CostEstimate(flops=4 * rows * rows * depth * cells, bytes_accessed=2 * rows * depth * cells, transcendentals=0),
        name="ham_inner",
    )(jnp.asarray(plane_weights(cells), jnp.bfloat16), boxes, potential)


def outer_kernel(count, place_ref, weights_ref, inner_ref, near_ref, far_ref, rims_ref, potential_ref, *refs):
    slab_refs, ham_ref = refs[:-1], refs[-1]
    depth, cells = potential_ref.shape
    position = place_ref[1]
    odd = position % 2 == 1
    edges = near_ref.shape[0] - EDGE * inner_ref.shape[0]
    near, far = near_ref[edges:], far_ref[edges:]
    none = jnp.zeros_like(near)
    below = jnp.where(position > 0, jnp.where(odd, near, far), none)
    above = jnp.where(position < count - 1, jnp.where(odd, far, near), none)
    weights = weights_ref[...]
    total = inner_ref[...]
    for side, (halo, start) in enumerate(((below, -EDGE), (above, depth))):
        rim_start = 0 if side == 0 else depth - 2 * EDGE

        def plane_at(plane):
            if 0 <= plane < depth:
                at = (plane - rim_start) * cells
                return rims_ref[side, :, at : at + cells]
            at = (plane - start) * halo.shape[0] // EDGE
            return halo[at : at + halo.shape[0] // EDGE]

        for plane in range(EDGE) if side == 0 else range(depth - EDGE, depth):
            image = image_of(plane_at, plane, weights, potential_ref[plane : plane + 1, :])
            total = total + lax.dot_general(plane_at(plane), image, NT, preferred_element_type=jnp.float32)
    ham_ref[...] = total
    rows = slab_refs[0].shape[0]
    for by, slab_ref in enumerate(slab_refs):
        at = pl.multiple_of(lax.bitwise_xor(position, by) * rows, rows)
        slab_ref[...] = ham_ref[pl.ds(at, rows), :]


def ham_outer(place, inner, near, far, rims, potential, count):
    rows = inner.shape[0]
    cells = potential.shape[1]
    vmem = pl.BlockSpec(memory_space=pltpu.VMEM)
    return pl.pallas_call(
        functools.partial(outer_kernel, count),
        out_shape=[jax.ShapeDtypeStruct((rows // count, rows), jnp.float32)] * count,
        in_specs=[pl.BlockSpec(memory_space=pltpu.SMEM)] + [vmem] * 6,
        out_specs=[vmem] * count,
        scratch_shapes=[pltpu.VMEM((rows, rows), jnp.float32)],
        compiler_params=pltpu.CompilerParams(vmem_limit_bytes=10 * MIB),
        name="ham_outer",
    )(place, jnp.asarray(plane_weights(cells), jnp.bfloat16), inner, near, far, rims, potential)


def outward_kernel(place_ref, blocks_ref, *refs):
    odd = place_ref[0] % 2 == 1
    count = refs[-1].shape[0]
    refs[-1][...] = jnp.where(odd, blocks_ref[:count], blocks_ref[-count:])


def outward(place, blocks, ahead):
    vmem = pl.BlockSpec(memory_space=pltpu.VMEM)
    return pl.pallas_call(
        outward_kernel,
        out_shape=jax.ShapeDtypeStruct((2,) + blocks.shape[1:], blocks.dtype),
        in_specs=[pl.BlockSpec(memory_space=pltpu.SMEM), vmem] + [ANY] * len(ahead),
        out_specs=vmem,
        compiler_params=pltpu.CompilerParams(vmem_limit_bytes=4 * MIB),
        name="outward",
    )(place, blocks, *ahead)


def pick_kernel(place_ref, own_ref, even_ref, odd_ref, *refs):
    even = place_ref[0] % 2 == place_ref[0] // 2 % 2
    refs[-1][0] = own_ref[...]
    refs[-1][1] = jnp.where(even, even_ref[...], odd_ref[...])


def pick(place, own, even, odd, ahead):
    vmem = pl.BlockSpec(memory_space=pltpu.VMEM)
    return pl.pallas_call(
        pick_kernel,
        out_shape=jax.ShapeDtypeStruct((2,) + own.shape, own.dtype),
        in_specs=[pl.BlockSpec(memory_space=pltpu.SMEM), vmem, vmem, vmem] + [ANY] * len(ahead),
        out_specs=vmem,
        compiler_params=pltpu.CompilerParams(vmem_limit_bytes=4 * MIB),
        name="pick",
    )(place, own, even, odd, *ahead)


def total_kernel(own_ref, across_ref, near_ref, far_ref, *refs):
    kept = own_ref.shape[0]
    whole = own_ref[...] + across_ref[...]
    for message_ref in (near_ref, far_ref):
        whole = whole + (message_ref[:kept].astype(jnp.float32) + message_ref[kept : 2 * kept].astype(jnp.float32))
    refs[-1][...] = whole


def total(own, across, near, far, ahead):
    vmem = pl.BlockSpec(memory_space=pltpu.VMEM)
    return pl.pallas_call(
        total_kernel,
        out_shape=jax.ShapeDtypeStruct(own.shape, own.dtype),
        in_specs=[vmem] * 4 + [ANY] * len(ahead),
        out_specs=vmem,
        compiler_params=pltpu.CompilerParams(vmem_limit_bytes=4 * MIB),
        name="total",
    )(own, across, near, far, *ahead)


def halves_of(value):
    high = value.astype(jnp.bfloat16)
    return high, (value - high.astype(jnp.float32)).astype(jnp.bfloat16)


def assemble_kernel(place_ref, *refs):
    part_refs, out_ref = refs[:-1], refs[-1]
    rows = part_refs[0].shape[1]
    for by, part_ref in enumerate(part_refs):
        at = pl.multiple_of(lax.bitwise_xor(place_ref[1], by) * rows, rows)
        for block in range(part_ref.shape[0]):
            high, low = halves_of(part_ref[block])
            out_ref[2 * block, pl.ds(at, rows), :] = high
            out_ref[2 * block + 1, pl.ds(at, rows), :] = low


def assemble(place, parts):
    blocks, rows, columns = parts[0].shape
    vmem = pl.BlockSpec(memory_space=pltpu.VMEM)
    return pl.pallas_call(
        assemble_kernel,
        out_shape=jax.ShapeDtypeStruct((2 * blocks, rows * len(parts), columns), jnp.bfloat16),
        in_specs=[pl.BlockSpec(memory_space=pltpu.SMEM)] + [vmem] * len(parts),
        out_specs=vmem,
        compiler_params=pltpu.CompilerParams(vmem_limit_bytes=16 * MIB),
        name="assemble",
    )(place, *parts)


def times(left, high, low):
    count = left.shape[0]
    left_high, left_low = halves_of(left)
    both = jnp.dot(jnp.concatenate([left_high, left_low], axis=0), high, preferred_element_type=jnp.float32)
    return both[:count] + both[count:] + jnp.dot(left_high, low, preferred_element_type=jnp.float32)


NEAR = (-1, 0, 1)
REACH = range(-2, 3)


def live_atoms(position, count, rotation):
    shifted = lax.rem(position // SF_ATOM - rotation + ATOMS_REG, ATOMS_REG)
    return (shifted < count).astype(jnp.float32)


def finish_kernel(parts, place_ref, count_ref, rotation_ref, *refs):
    part_refs, out_ref = refs[:parts], refs[-1]
    rows, columns = out_ref.shape
    count, rotation = count_ref[place_ref[0]], rotation_ref[place_ref[0]]
    own_rows = lax.broadcasted_iota(jnp.int32, (rows, 1), 0) + place_ref[1] * rows
    lanes = lax.broadcasted_iota(jnp.int32, (1, columns), 1)
    kept = live_atoms(own_rows, count, rotation) * live_atoms(lanes, count, rotation)
    out_ref[...] = sum(ref[...] for ref in part_refs) * kept


def finish(place, live_count, rotation, parts, ahead):
    smem, vmem = pl.BlockSpec(memory_space=pltpu.SMEM), pl.BlockSpec(memory_space=pltpu.VMEM)
    return pl.pallas_call(
        functools.partial(finish_kernel, len(parts)),
        out_shape=jax.ShapeDtypeStruct(parts[0].shape, jnp.float32),
        in_specs=[smem] * 3 + [vmem] * len(parts) + [ANY] * len(ahead),
        out_specs=vmem,
        compiler_params=pltpu.CompilerParams(vmem_limit_bytes=4 * MIB),
        name="finish",
    )(place, live_count, rotation, *parts, *ahead)


def purify_kernel(place_ref, count_ref, rotation_ref, bond_ref, slab_ref, *refs):
    block_refs, out_ref = refs[4:9], refs[9]
    own, (core, cross), even_pair, odd_pair = (ref[...] for ref in refs[:4])
    odd_region, odd_chip = place_ref[0] % 2 == 1, place_ref[0] // 2 % 2 == 1
    shares = {
        -2: jnp.where(odd_chip, even_pair, odd_pair),
        -1: jnp.where(odd_region, core, cross),
        0: own,
        1: jnp.where(odd_region, cross, core),
        2: jnp.where(odd_chip, odd_pair, even_pair),
    }
    regions = count_ref.shape[0]
    rows, columns = slab_ref.shape[1:]

    def at(e):
        return lax.rem(place_ref[0] + e + regions, regions)

    bonds = {e: bond_ref[at(e)].astype(jnp.float32) for e in range(-2, 2)}
    lanes = lax.broadcasted_iota(jnp.int32, (1, columns), 1)
    live = {e: live_atoms(lanes, count_ref[at(e)], rotation_ref[at(e)]) for e in REACH}
    own_rows = lax.broadcasted_iota(jnp.int32, (rows, 1), 0) + place_ref[1] * rows
    row_live = live_atoms(own_rows, count_ref[at(0)], rotation_ref[at(0)])

    def pattern(region, offset):
        return 1.0 if offset == 0 else bonds[region + min(offset, 0)]

    overlap = {e: halves_of(unpacked(shares[e])) for e in REACH}

    def by_block(left, region, offset):
        part = lambda ref, block: (ref[2 * block], ref[2 * block + 1])
        choose = lambda odd, yes, no: [jnp.where(odd, a, b) for a, b in zip(yes, no)]
        own_ref, core_ref, cross_ref, beyond_ref, behind_ref = block_refs
        if region == 0:
            return times(left, *part(own_ref, offset + 1))
        if abs(region) == 1:
            core_part, cross_part = part(core_ref, offset + 1), part(cross_ref, offset + 1)
            return times(left, *(choose(odd_region, core_part, cross_part) if region < 0 else choose(odd_region, cross_part, core_part)))
        beyond_part, behind_part = part(beyond_ref, 0), part(behind_ref, 0)
        return times(left, *(choose(odd_region, behind_part, beyond_part) if region < 0 else choose(odd_region, beyond_part, behind_part)))

    first = {e: times(slab_ref[e + 1] * (live[e] * pattern(0, e)), *overlap[e]) * live[e] for e in NEAR}
    chain = {(e, f): by_block(first[e], e, f) * (live[e + f] * pattern(e, f)) for e in NEAR for f in NEAR}
    longer = {}
    for h in REACH:
        members = [(e, h - e) for e in NEAR if h - e in NEAR]
        product = times(jnp.concatenate([chain[m] for m in members], axis=0), *overlap[h]) * live[h]
        for place, member in enumerate(members):
            longer[member] = product[place * rows : (place + 1) * rows]
    for d in NEAR:
        second = sum(chain[e, d - e] for e in NEAR if d - e in NEAR)
        triple = jnp.zeros_like(second)
        for h in REACH:
            if d - h not in NEAR:
                continue
            left = sum(longer[e, h - e] * pattern(e, d - e) for e in NEAR if h - e in NEAR and d - e in NEAR)
            triple = triple + by_block(left * pattern(h, d - h), h, d - h)
        out_ref[d + 1] = (3.0 * second - 2.0 * triple) * (row_live * (live[d] * pattern(0, d)))


def purify(place, live_count, rotation, bond, slab, overlaps, blocks):
    smem, vmem = pl.BlockSpec(memory_space=pltpu.SMEM), pl.BlockSpec(memory_space=pltpu.VMEM)
    return pl.pallas_call(
        purify_kernel,
        out_shape=jax.ShapeDtypeStruct(slab.shape, jnp.float32),
        in_specs=[smem] * 4 + [vmem] * 10,
        out_specs=vmem,
        compiler_params=pltpu.CompilerParams(vmem_limit_bytes=24 * MIB),
        name="purify",
    )(place, live_count, rotation, bond, slab, *overlaps, *blocks)


def swapped(block, axis, partner):
    count = lax.axis_size(axis)
    return lax.ppermute(block, axis, [(at, partner(at) % count) for at in range(count)])


def same_chip(at):
    return at ^ 1


def next_region_across(at):
    return at + 1 if at % 2 else at - 1


def even_chip_with_next(at):
    return at - 2 if at // 2 % 2 else at + 2


def odd_chip_with_next(at):
    return at + 2 if at // 2 % 2 else at - 2


def shards(psi, potential, kernel, live_count, rotation, bond):
    atom_count, kern_count = lax.axis_size("atoms"), lax.axis_size("kern")
    depth, cells = psi.shape[2:]
    place = jnp.stack([lax.axis_index("atoms"), lax.axis_index("kern")]).astype(jnp.int32)
    along_kern = [lambda at, by=by: at ^ by for by in range(kern_count)]

    got = lax.all_to_all(psi, "atoms", split_axis=0, concat_axis=0, tiled=True)

    slab = kernel[0]
    own = assemble(place, [slab] + [swapped(slab, "kern", partner) for partner in along_kern[1:]])
    core = swapped(own, "atoms", same_chip)
    cross = swapped(own, "atoms", next_region_across)
    away = [(at, (at - 2 if at % 2 else at + 2) % atom_count) for at in range(atom_count)]
    beyond = lax.ppermute(outward(place, own, ()), "atoms", away)
    boxes = got.reshape(-1, depth, cells)
    share, near, far = gram(place, boxes, (own, core))
    opposite = swapped(share, "kern", along_kern[2])
    near, far = swapped(near, "kern", along_kern[1]), swapped(far, "kern", along_kern[3])
    inner, rims = ham_inner(boxes, potential[0])
    slabs = ham_outer(place, inner, near, far, rims, potential[0], kern_count)
    inter = total(share, opposite, near, far, (slabs[0], cross, beyond))
    sent = outward(place, cross, (inter,))
    behind = swapped(sent, "atoms", same_chip)

    two_even, two_odd = swapped(inter, "atoms", even_chip_with_next), swapped(inter, "atoms", odd_chip_with_next)
    parts = [slabs[0]] + [swapped(part, "kern", partner) for part, partner in zip(slabs[1:], along_kern[1:])]
    picked = pick(place, inter, two_even, two_odd, (sent, *parts[:-1]))
    from_core = swapped(picked, "atoms", same_chip)
    ham_mine = finish(place, live_count, rotation, parts, (picked,))
    overlaps = [inter, from_core, two_even, two_odd]

    blocks = [own, core, cross, beyond, behind]
    kernel_new = purify(place, live_count, rotation, bond, slab, overlaps, blocks)
    return (ham_mine[None], kernel_new[None])


def solution(mesh):
    in_specs = (
        P("atoms", None, "kern", None),
        P("atoms", "kern", None),
        P("atoms", None, "kern", None),
        P(),
        P(),
        P(),
    )
    out_specs = (P("atoms", "kern", None), P("atoms", None, "kern", None))
    return jax.shard_map(shards, mesh=mesh, in_specs=in_specs, out_specs=out_specs, check_vma=False)
```
